32 devices in a mesh: gx: 8 (over z, core), gy: 4 (over y, x).
Axes of the slice: x: 2, y: 2, z: 4, core: 2. Of those that a mesh axis runs over, the one named last changes fastest.
Arguments:
- velocity: float32 [3, 6144, 2048], P(None, 'gx', 'gy'), may hold values from -6 to 6
- row_owner: int32 [8, 16], P('gx'), may hold values from 0 to 3, as said below
- cell_list: int32 [4, 16384], P(None, ('gx', 'gy')), may hold values from 0 to 786431, as said below
- weights: float32 [4, 16384], P(None, ('gx', 'gy')), may hold values from 0.05 to 0.5
- offsets: float32 [16384], P(('gx', 'gy')), may hold values from -0.5 to 0.5
- relax_rate: float32 [16384], P(('gx', 'gy')), may hold values from 0.05 to 0.8
- particle_velocity: float32 [3, 16384], P(None, ('gx', 'gy')), may hold values from -6 to 6
- live_counts: int32 [128], P(('gx', 'gy')), may hold values from 1 to 128, as said below
Outputs:
- gradient: float32 [3, 6144, 2048], P(None, 'gx', 'gy')
- fluid_at_particle: float32 [3, 16384], P(None, ('gx', 'gy'))
- updated_velocity: float32 [3, 16384], P(None, ('gx', 'gy'))
The draws below stay inside these ranges and needn't reach their ends.
Inputs may be any that keep to these rules, and one draw needn't show every extreme that they name: `row_owner`: for every gx index and every gy index, at most 2 of that device's 4 row blocks name one owner; in every row of devices along gy one owner is named by exactly 2 blocks of every device; every owner is named by some block of the row. `cell_list`: every entry decodes as in the reference program to a block that exists; the 4 cells of one particle share q. `live_counts`: the live particles of a block are its first slots.
All inputs are finite; a program needn't handle non-finite values.
Results may differ from the reference program's by a relative error of at most 0.0029.
Values may be sent and summed in bfloat16 or wider, within the bound.
No kernel may reach another device: no remote copies, remote signals or barrier semaphores. Data moves between devices by JAX's collectives and lax.ppermute only.
A program may use at most 128 MiB of HBM per device.

```python
import math
import jax
import jax.numpy as jnp

NX = 6144
CX = 768
LINES = 2048
ROWB = 128
NBLK_DEV = 4
NBLK = 16
CAP = 2
PART_DEV = 512
PSIZE = 128
PBLK_DEV = 4
PARTS_SIZE = 16384
STEN = 4
N_GX = 8
N_GY = 4
DEVICES = 32


def route_table(key):
    base_key = jax.random.fold_in(key, 7001)
    key_hot, key_order = jax.random.split(base_key)
    hot_owner = jax.random.randint(key_hot, (N_GX, 1, 1), 0, N_GY)
    sender = jnp.arange(N_GY)[None, :, None]
    position = jnp.arange(NBLK_DEV)[None, None, :]
    spread = (sender + position - CAP) % (N_GY - 1)
    owner_seq = jnp.where(position < CAP, hot_owner, (hot_owner + 1 + spread) % N_GY)
    owner_seq = jnp.broadcast_to(owner_seq, (N_GX, N_GY, NBLK_DEV))
    scores = jax.random.randint(key_order, (N_GX, N_GY, NBLK_DEV), 0, 1 << 20) * NBLK_DEV + position
    shuffle = jnp.argsort(scores, axis=-1)
    inverse = jnp.argsort(shuffle, axis=-1)
    routes = jnp.take_along_axis(owner_seq, inverse, -1)
    return (routes.reshape(N_GX, NBLK).astype(jnp.int32), hot_owner)


def draw_row_owner(key, part):
    routes, hot_owner = route_table(key)
    return routes


def draw_cell_list(key, part):
    routes, hot_owner = route_table(key)
    pick_key = jax.random.fold_in(key, 7002)
    key_block, key_line, key_cell = jax.random.split(pick_key, 3)
    particle_ids = jnp.arange(PARTS_SIZE)
    device_ids = particle_ids // PART_DEV
    column_ids = device_ids // N_GY
    owner_ids = device_ids % N_GY
    to_owner = (routes[column_ids] == owner_ids[:, None]).astype(jnp.int32)
    running = jnp.cumsum(to_owner, 1)
    available = running[:, -1]
    chosen_rank = jax.random.randint(key_block, (PARTS_SIZE,), 0, available)
    block_id = jnp.sum((running <= chosen_rank[:, None]).astype(jnp.int32), 1)
    sender = block_id // NBLK_DEV
    ordinal = jnp.arange(NBLK)[None, :]
    before = (ordinal < block_id[:, None]) & (ordinal >= (sender * NBLK_DEV)[:, None])
    within = jnp.sum(to_owner * before.astype(jnp.int32), 1)
    slot_ids = sender * CAP + within
    line_index = jax.random.randint(key_line, (PARTS_SIZE,), 0, ROWB)
    x_index = jax.random.randint(key_cell, (PARTS_SIZE,), 0, CX)
    top_particle = hot_owner[0, 0, 0] * PART_DEV
    slot_ids = slot_ids.at[top_particle].set(N_GY * CAP - 1).at[top_particle + 1].set(0)
    line_index = line_index.at[top_particle].set(ROWB - 1).at[top_particle + 1].set(0)
    x_index = x_index.at[top_particle].set(CX - 1).at[top_particle + 1].set(0)
    stencil = jnp.arange(STEN)[:, None]
    x_cells = (x_index[None] + stencil % 2) % CX
    line_cells = (line_index[None] + stencil // 2) % ROWB
    return ((slot_ids[None] * ROWB + line_cells) * CX + x_cells).astype(jnp.int32)


def draw_live_counts(key, part):
    base_key = jax.random.fold_in(key, 7003)
    key_level, key_raw = jax.random.split(base_key)
    load_level = jax.random.randint(key_level, (DEVICES, 1), 1, 5)
    raw_draw = jax.random.randint(key_raw, (DEVICES, PBLK_DEV), 0, PSIZE)
    counts = (1 + raw_draw * load_level // 4).reshape(-1)
    return counts.at[0].set(PSIZE).astype(jnp.int32)


def shard_levels(stream_key, extent, pieces, least, top_value):
    def one(axis_at, parts):
        draws = jax.random.uniform(jax.random.fold_in(jax.random.fold_in(stream_key, 6), axis_at), (parts,), jnp.float32, least / len(pieces), top_value / len(pieces))
        return jnp.repeat(jnp.exp(draws), extent[axis_at] // parts).reshape((-1,) + (1,) * (len(extent) - axis_at - 1))

    factor_of = one(*pieces[0])
    for cut in pieces[1:]:
        factor_of = factor_of * one(*cut)
    return factor_of


def normal_values(own_key, dims, deviation, reach, cuts=(), held_as=jnp.bfloat16):
    values = deviation * jax.random.normal(own_key, dims, jnp.float32)
    if cuts:
        values = values * shard_levels(own_key, dims, cuts, -0.22, 0.18)
    return jnp.clip(values, -reach, reach).astype(held_as)


def setup_inputs(seed: int = 0) -> dict:
    keys = jax.random.split(jax.random.key(seed), 9)
    velocity = normal_values(keys[0], (3, NX, LINES), 1.0, 6.0, ((1, 8), (2, 4)), jnp.float32)
    row_owner = draw_row_owner(jax.random.fold_in(keys[8], 71), 0)
    cell_list = draw_cell_list(jax.random.fold_in(keys[8], 71), 0)
    weights = jnp.clip(0.05 + 0.45 * jax.random.uniform(keys[3], (STEN, PARTS_SIZE), jnp.float32) ** shard_levels(keys[3], (STEN, PARTS_SIZE), ((1, 32),), -0.2, 0.2), 0.05, 0.5)
    offsets = jnp.clip(jax.random.uniform(keys[4], (PARTS_SIZE,), jnp.float32, -0.5, 0.5) * shard_levels(keys[4], (PARTS_SIZE,), ((0, 32),), -0.4, 0.0), -0.5, 0.5)
    relax_rate = jnp.clip(jnp.exp(math.log(0.8) - 2.7725887 * jax.random.uniform(keys[5], (PARTS_SIZE,), jnp.float32) ** shard_levels(keys[5], (PARTS_SIZE,), ((0, 32),), -0.2, 0.2)), 0.05, 0.8)
    particle_velocity = normal_values(keys[6], (3, PARTS_SIZE), 1.0, 6.0, ((1, 32),), jnp.float32)
    live_counts = draw_live_counts(jax.random.fold_in(keys[8], 71), 0)
    return {"velocity": velocity, "row_owner": row_owner, "cell_list": cell_list, "weights": weights, "offsets": offsets, "relax_rate": relax_rate, "particle_velocity": particle_velocity, "live_counts": live_counts}


def stencil_sum(values, weights, offsets):
    carried = values[:3].astype(jnp.float32)
    slopes = values[3:].astype(jnp.float32)
    return jnp.sum(weights[None] * (carried + offsets[None, None] * slopes), 1)


def reference(velocity, row_owner, cell_list, weights, offsets, relax_rate, particle_velocity, live_counts):
    wavenumber = 2.0 * math.pi * jnp.fft.fftfreq(NX)
    modified_wave = ((14.0 / 9.0) * jnp.sin(wavenumber) + (1.0 / 18.0) * jnp.sin(2.0 * wavenumber)) / (1.0 + (2.0 / 3.0) * jnp.cos(wavenumber))
    derivatives = []
    for channel in range(3):
        spectrum = jnp.fft.fft(velocity[channel], axis=0)
        derivatives.append(jnp.real(jnp.fft.ifft(1j * modified_wave[:, None] * spectrum, axis=0)).astype(jnp.float32))
    gradient = jnp.stack(derivatives)
    fields = jnp.concatenate([velocity, gradient], 0).astype(jnp.bfloat16)
    particle_ids = jnp.arange(PARTS_SIZE).astype(jnp.int32)
    device_ids = particle_ids // PART_DEV
    column_ids = device_ids // N_GY
    owner_ids = device_ids % N_GY
    x_index = cell_list % CX
    remainder = cell_list // CX
    line_index = remainder % ROWB
    slot_ids = remainder // ROWB
    sender = slot_ids // CAP
    within = slot_ids % CAP
    block_ids = sender[..., None] * NBLK_DEV + jnp.arange(NBLK_DEV).astype(jnp.int32)
    owners_seen = row_owner[column_ids[None, :, None], block_ids]
    running = jnp.cumsum((owners_seen == owner_ids[None, :, None]).astype(jnp.int32), -1)
    position = jnp.sum((running <= within[..., None]).astype(jnp.int32), -1)
    cell_line = (sender * NBLK_DEV + position) * ROWB + line_index
    cell_x = column_ids[None, :] * CX + x_index
    values = fields[:, cell_x, cell_line]
    raw = stencil_sum(values, weights, offsets)
    alive = (jnp.arange(PSIZE)[None, :] < live_counts[:, None]).reshape(PARTS_SIZE)
    fluid_at_particle = jnp.where(alive[None], raw, 0.0)
    updated_velocity = jnp.where(alive[None], particle_velocity + relax_rate[None] * (fluid_at_particle - particle_velocity), particle_velocity)
    return gradient, fluid_at_particle, updated_velocity
```

```python
import math

import jax
import jax.numpy as jnp
import numpy as np
from jax import lax
from jax.experimental import pallas as pl
from jax.experimental.pallas import tpu as pltpu
from jax.sharding import PartitionSpec as P

ROWB = 128
PSIZE = 128
STEN = 4
EDGE = 32
ROWS = 192
CHUNK = 64
R_DECAY = (3.0 - math.sqrt(5.0)) / 2.0
F32 = jnp.float32
BF16 = jnp.bfloat16


def kernel_taps(reach):
    level = 3.0 / math.sqrt(5.0)

    def inverse(n):
        return level * (-R_DECAY) ** abs(n)

    taps = np.zeros(reach + 1)
    for n in range(reach + 1):
        taps[n] = (7.0 / 9.0) * (inverse(n + 1) - inverse(n - 1)) + (1.0 / 36.0) * (
            inverse(n + 2) - inverse(n - 2)
        )
    return taps


TAPS = kernel_taps(300)
TAIL = TAPS[2] / R_DECAY**2
FIRST = TAPS[1] + TAIL * R_DECAY


def split(values, terms):
    parts = []
    for _ in range(terms):
        part = values.astype(BF16)
        parts.append(part)
        values = values - part.astype(F32)
    return parts


def toeplitz(offset, rows, window):
    distance = offset + np.arange(rows)[:, None] - np.arange(window)[None, :]
    full = np.sign(distance) * TAPS[np.abs(distance)]
    high = full.astype(BF16)
    low = (full - high.astype(np.float64)).astype(BF16)
    return np.stack([high, low])


def edge_state(rows, from_first):
    index = lax.broadcasted_iota(jnp.int32, rows.shape, 0)
    steps = index + 1 if from_first else EDGE - index
    parity = 1.0 - 2.0 * (steps & 1).astype(F32)
    decay = parity * jnp.exp(steps.astype(F32) * math.log(R_DECAY))
    return jnp.sum(rows * decay, 0, keepdims=True)


def prep_body(x_cells, live, head, tail, cells, weights, offsets, to_right, to_left, request):
    zero = jnp.zeros((2, head.shape[2]), F32)
    to_left[...] = jnp.concatenate(
        [edge_state(head[c], True) for c in range(3)] + [head[c, 0:1, :] for c in range(3)] + [zero], 0
    )
    to_right[...] = jnp.concatenate(
        [edge_state(tail[c], False) for c in range(3)]
        + [tail[c, EDGE - 1 : EDGE, :] for c in range(3)]
        + [zero],
        0,
    )
    cell = cells[...]
    slots = cell.shape[1]
    row = jnp.floor((cell.astype(F32) + 0.5) * (1.0 / x_cells)).astype(jnp.int32)
    x = cell - row * x_cells
    line = row & (ROWB - 1)
    slot = (row >> 7)[0:1]
    lane = lax.broadcasted_iota(jnp.int32, (1, slots), 1)
    limit = jnp.zeros((1, slots), jnp.int32)
    for k in range(slots // PSIZE):
        limit = jnp.where(lane // PSIZE == k, live[k], limit)
    alive = lane % PSIZE < limit
    key = jnp.where(alive, slot, -1).astype(F32)
    w_high, w_low = split(weights[...], 2)
    o_high, o_low = split(offsets[...].reshape(1, slots), 2)
    request[...] = jnp.concatenate(
        [
            (x >> 3).astype(F32),
            (x & 7).astype(F32),
            line.astype(F32),
            w_high.astype(F32),
            w_low.astype(F32),
            o_high.astype(F32),
            o_low.astype(F32),
            key,
            jnp.zeros((9, slots), F32),
        ],
        0,
    ).astype(BF16)


def derivative_body(plan, v_ref, t_ref, g_ref, fv_ref, fg_ref, edge_ref):
    window = t_ref.shape[3]
    high, low = split(v_ref[0], 2)
    lanes = high.shape[1]
    x_cells = high.shape[0]
    for k in range(lanes // ROWB):
        fv_ref[0, k] = high[:, k * ROWB : (k + 1) * ROWB]
    for row, start, kind in plan:
        hi = high[start : start + window]
        lo = low[start : start + window]
        t_high, t_low = t_ref[kind, 0], t_ref[kind, 1]
        out = (
            jnp.dot(t_high, hi, preferred_element_type=F32)
            + jnp.dot(t_high, lo, preferred_element_type=F32)
            + jnp.dot(t_low, hi, preferred_element_type=F32)
        )
        g_ref[0, row : row + ROWS] = out
        rounded = out.astype(BF16)
        for k in range(lanes // ROWB):
            fg_ref[0, k, row : row + ROWS] = rounded[:, k * ROWB : (k + 1) * ROWB]
        if row == 0:
            edge_ref[0, :EDGE] = out[:EDGE]
        if row + ROWS == x_cells:
            edge_ref[0, EDGE:] = out[ROWS - EDGE :]


def edge_fix(rows, state, plane, is_left):
    index = lax.broadcasted_iota(jnp.int32, rows.shape, 0)
    steps = index if is_left else EDGE - 1 - index
    parity = 1.0 - 2.0 * (steps & 1).astype(F32)
    decay = parity * jnp.exp(steps.astype(F32) * math.log(R_DECAY))
    sign = 1.0 if is_left else -1.0
    return rows + (sign * TAIL) * decay * state + jnp.where(steps == 0, sign * FIRST, 0.0) * plane


def lookup_body(
    owners, xor, owner_ref, fv_ref, fg_ref, edge_ref, left_ref, right_ref, *refs
):
    request_refs = refs[:owners]
    grad_in = refs[owners]
    grad_out = refs[owners + 1]
    out_refs = refs[owners + 2 : 2 * owners + 2]
    requests, fixed, ranks, counts, totals, sems = refs[2 * owners + 2 :]
    del grad_in
    step = pl.program_id(0)
    blocks = pl.num_programs(0)
    me = lax.axis_index("gy")
    capacity = 2
    slots = requests.shape[2]
    groups = slots // ROWB
    x_cells = fv_ref.shape[2]
    block_total = 4

    def peer_of(block):
        owner = owner_ref[0, me * block_total + block]
        return (owner ^ me) if xor else lax.rem(owner - me + owners, owners)

    def edge_copies():
        return (
            pltpu.make_async_copy(
                fixed.at[:, pl.ds(0, EDGE)], grad_out.at[:, pl.ds(0, EDGE)], sems.at[0]
            ),
            pltpu.make_async_copy(
                fixed.at[:, pl.ds(EDGE, EDGE)],
                grad_out.at[:, pl.ds(x_cells - EDGE, EDGE)],
                sems.at[1],
            ),
        )

    @pl.when(step == 0)
    def _():
        for c in range(3):
            fixed[c, :EDGE] = edge_fix(
                edge_ref[c, :EDGE], left_ref[c : c + 1], left_ref[c + 3 : c + 4], True
            )
            fixed[c, EDGE:] = edge_fix(
                edge_ref[c, EDGE:], right_ref[c : c + 1], right_ref[c + 3 : c + 4], False
            )
        for copy in edge_copies():
            copy.start()
        for k in range(owners):
            requests[k] = request_refs[k][...]
            totals[k] = jnp.zeros(totals.shape[1:], F32)
        matched = []
        for block in range(block_total):
            peer = peer_of(block)
            rank = jnp.int32(0)
            for earlier in range(block):
                rank += (peer_of(earlier) == peer).astype(jnp.int32)
            key = requests[peer, 16:32, :].astype(F32)[6:7]
            matched.append(jnp.where(key == (me * capacity + rank).astype(F32), 1.0, 0.0))
        stacked = jnp.concatenate(
            [m[:, k * ROWB : (k + 1) * ROWB] for m in matched for k in range(groups)], 0
        )
        upto = lax.broadcasted_iota(jnp.int32, (ROWB, ROWB), 0) <= lax.broadcasted_iota(
            jnp.int32, (ROWB, ROWB), 1
        )
        running = jnp.dot(
            stacked.astype(BF16), jnp.where(upto, 1.0, 0.0).astype(BF16), preferred_element_type=F32
        )
        for block in range(block_total):
            before = jnp.zeros((1, 1), F32)
            pieces = []
            for k in range(groups):
                r = block * groups + k
                here = stacked[r : r + 1]
                line = running[r : r + 1]
                pieces.append(jnp.where(here > 0.5, line - 1.0 + before, -1.0))
                before = before + line[:, ROWB - 1 : ROWB]
            ranks[block] = jnp.concatenate(pieces, 1)
            counts[block] = before[0, 0].astype(jnp.int32)

    peer = peer_of(step)
    lanes_at = pl.ds(pl.multiple_of(step * ROWB, ROWB), ROWB)
    count = counts[step]
    lane = lax.broadcasted_iota(jnp.int32, (CHUNK, ROWB), 1).astype(F32)
    lane_x = lax.broadcasted_iota(jnp.int32, (CHUNK, x_cells), 1).astype(F32)
    tables = [fv_ref[c, 0] for c in range(3)] + [
        jnp.concatenate(
            [
                fixed[c, :EDGE, lanes_at].astype(BF16),
                fg_ref[c, 0, EDGE : x_cells - EDGE],
                fixed[c, EDGE:, lanes_at].astype(BF16),
            ],
            0,
        )
        for c in range(3)
    ]
    table = jnp.concatenate(tables, 1)

    def chunk(i, carry):
        place = (lax.broadcasted_iota(jnp.int32, (CHUNK, slots), 0) + i * CHUNK).astype(F32)
        chosen = jnp.where(ranks[step] == place, 1.0, 0.0).astype(BF16)
        data = lax.dot_general(
            chosen, requests[peer], (((1,), (1,)), ((), ())), preferred_element_type=F32
        )
        picks, masks = [], []
        for s in range(STEN):
            x = data[:, s : s + 1] * 8.0 + data[:, 4 + s : 5 + s]
            weight = data[:, 12 + s : 13 + s] + data[:, 16 + s : 17 + s]
            picks.append(jnp.where(lane_x == x, 1.0, 0.0).astype(BF16))
            masks.append(jnp.where(lane == data[:, 8 + s : 9 + s], weight, 0.0))
        offset = data[:, 20:21] + data[:, 21:22]
        rows = jnp.dot(jnp.concatenate(picks, 0), table, preferred_element_type=F32)
        sums = []
        for c in range(6):
            total = jnp.zeros((CHUNK, ROWB), F32)
            for s in range(STEN):
                total += masks[s] * rows[s * CHUNK : (s + 1) * CHUNK, c * ROWB : (c + 1) * ROWB]
            sums.append(total)
        value = jnp.zeros((CHUNK, ROWB), F32)
        for c in range(3):
            mixed = jnp.sum(sums[c] + offset * sums[3 + c], 1, keepdims=True)
            for k, part in enumerate(split(mixed, 3)):
                value = jnp.where(lane == float(k * 4 + c), part.astype(F32), value)
        back = jnp.transpose(value)[:16].astype(BF16)
        placed = jnp.dot(back, chosen, preferred_element_type=F32)
        totals[peer] += placed
        return carry

    lax.fori_loop(0, (count + CHUNK - 1) // CHUNK, chunk, 0)

    @pl.when(step == blocks - 1)
    def _():
        for k in range(owners):
            total = totals[k]
            both = total[0:8] + pltpu.roll(total[0:8], 4, 0) + total[8:16]
            out_refs[k][...] = both
        for copy in edge_copies():
            copy.wait()


def final_body(live, relax, particle, *refs):
    parts, (fluid_ref, updated_ref) = refs[:-2], refs[-2:]
    raw = parts[0][0:3]
    for part in parts[1:]:
        raw = raw + part[0:3]
    slots = raw.shape[1]
    lane = lax.broadcasted_iota(jnp.int32, (3, slots), 1)
    limit = jnp.zeros((3, slots), jnp.int32)
    for k in range(slots // PSIZE):
        limit = jnp.where(lane // PSIZE == k, live[k], limit)
    alive = lane % PSIZE < limit
    fluid = jnp.where(alive, raw, 0.0)
    velocity = particle[...]
    fluid_ref[...] = fluid
    updated_ref[...] = jnp.where(
        alive, velocity + relax[...].reshape(1, slots) * (fluid - velocity), velocity
    )


def sent(values, axis, pairs):
    return lax.ppermute(values, axis, pairs)


def per_device(
    velocity, row_owner, cell_list, weights, offsets, relax_rate, particle_velocity, live_counts
):
    components, x_cells, lines = velocity.shape
    slots = weights.shape[1]
    columns = lax.axis_size("gx")
    owners = lax.axis_size("gy")
    blocks = lines // ROWB
    xor = owners & (owners - 1) == 0
    vmem = pl.BlockSpec(memory_space=pltpu.VMEM)
    smem = pl.BlockSpec(memory_space=pltpu.SMEM)
    anywhere = pl.BlockSpec(memory_space=pl.ANY)
    limit = 48 * 1024 * 1024

    last = x_cells // EDGE - 1
    one = lambda shape: pl.BlockSpec(shape, lambda i: (0,) * len(shape))
    to_right, to_left, request = pl.pallas_call(
        lambda *refs: prep_body(x_cells, *refs),
        grid=(1,),
        in_specs=[
            smem,
            pl.BlockSpec((3, EDGE, lines), lambda i: (0, 0, 0)),
            pl.BlockSpec((3, EDGE, lines), lambda i: (0, last, 0)),
            one((STEN, slots)),
            one((STEN, slots)),
            one((slots,)),
        ],
        out_specs=[one((8, lines)), one((8, lines)), one((32, slots))],
        out_shape=[
            jax.ShapeDtypeStruct((8, lines), F32),
            jax.ShapeDtypeStruct((8, lines), F32),
            jax.ShapeDtypeStruct((32, slots), BF16),
        ],
        name="prepare",
    )(live_counts, velocity, velocity, cell_list, weights, offsets)

    from_left = sent(to_right, "gx", [(i, (i + 1) % columns) for i in range(columns)])
    from_right = sent(to_left, "gx", [((i + 1) % columns, i) for i in range(columns)])

    def peer(i, k):
        return i ^ k if xor else (i + k) % owners

    requests = [request] + [
        sent(request, "gy", [(peer(i, k), i) for i in range(owners)]) for k in range(1, owners)
    ]

    window = min(256, x_cells)
    plan, kinds = [], []
    for row in range(0, x_cells, ROWS):
        start = min(max(row - EDGE, 0), x_cells - window)
        if row - start not in kinds:
            kinds.append(row - start)
        plan.append((row, start, kinds.index(row - start)))
    matrices = jnp.asarray(np.stack([toeplitz(o, ROWS, window) for o in kinds]))
    tile = 256
    per_tile = tile // ROWB
    gradient, table_v, table_g, edges = pl.pallas_call(
        lambda *refs: derivative_body(plan, *refs),
        grid=(components, lines // tile),
        in_specs=[
            pl.BlockSpec((1, x_cells, tile), lambda c, t: (c, 0, t)),
            pl.BlockSpec(matrices.shape, lambda c, t: (0, 0, 0, 0)),
        ],
        out_specs=[
            pl.BlockSpec((1, x_cells, tile), lambda c, t: (c, 0, t)),
            pl.BlockSpec((1, per_tile, x_cells, ROWB), lambda c, t: (c, t, 0, 0)),
            pl.BlockSpec((1, per_tile, x_cells, ROWB), lambda c, t: (c, t, 0, 0)),
            pl.BlockSpec((1, 2 * EDGE, tile), lambda c, t: (c, 0, t)),
        ],
        out_shape=[
            jax.ShapeDtypeStruct(velocity.shape, F32),
            jax.ShapeDtypeStruct((components, blocks, x_cells, ROWB), BF16),
            jax.ShapeDtypeStruct((components, blocks, x_cells, ROWB), BF16),
            jax.ShapeDtypeStruct((components, 2 * EDGE, lines), F32),
        ],
        compiler_params=pltpu.CompilerParams(vmem_limit_bytes=limit),
        cost_estimate=pl.CostEstimate(
            flops=6 * window * velocity.size, bytes_accessed=14 * velocity.size, transcendentals=0
        ),
        name="derivative",
    )(velocity, matrices)

    outs = pl.pallas_call(
        lambda *refs: lookup_body(owners, xor, *refs),
        grid=(blocks,),
        in_specs=[
            smem,
            pl.BlockSpec((components, 1, x_cells, ROWB), lambda b: (0, b, 0, 0)),
            pl.BlockSpec((components, 1, x_cells, ROWB), lambda b: (0, b, 0, 0)),
            one((components, 2 * EDGE, lines)),
            one((8, lines)),
            one((8, lines)),
        ]
        + [one((32, slots))] * owners
        + [anywhere],
        out_specs=[anywhere] + [one((8, slots))] * owners,
        out_shape=[jax.ShapeDtypeStruct(velocity.shape, F32)]
        + [jax.ShapeDtypeStruct((8, slots), F32)] * owners,
        scratch_shapes=[
            pltpu.VMEM((owners, 32, slots), BF16),
            pltpu.VMEM((components, 2 * EDGE, lines), F32),
            pltpu.VMEM((blocks, 1, slots), F32),
            pltpu.SMEM((blocks,), jnp.int32),
            pltpu.VMEM((owners, 16, slots), F32),
            pltpu.SemaphoreType.DMA((2,)),
        ],
        input_output_aliases={6 + owners: 0},
        compiler_params=pltpu.CompilerParams(vmem_limit_bytes=limit),
        cost_estimate=pl.CostEstimate(
            flops=2 * 768 * 6 * x_cells * 1024, bytes_accessed=4 * velocity.size, transcendentals=0
        ),
        name="lookup",
    )(row_owner, table_v, table_g, edges, from_left, from_right, *requests, gradient)
    gradient, partials = outs[0], outs[1:]

    returned = [partials[0]] + [
        sent(partials[k], "gy", [(i, peer(i, k)) for i in range(owners)]) for k in range(1, owners)
    ]
    shape = jax.ShapeDtypeStruct((3, slots), F32)
    fluid, updated = pl.pallas_call(
        final_body,
        grid=(1,),
        in_specs=[smem, one((slots,)), one((3, slots))] + [one((8, slots))] * owners,
        out_specs=[one((3, slots))] * 2,
        out_shape=[shape, shape],
        name="finish",
    )(live_counts, relax_rate, particle_velocity, *returned)
    return (gradient, fluid, updated)


def solution(mesh):
    return jax.shard_map(
        per_device,
        mesh=mesh,
        in_specs=(
            P(None, "gx", "gy"),
            P("gx", None),
            P(None, ("gx", "gy")),
            P(None, ("gx", "gy")),
            P(("gx", "gy")),
            P(("gx", "gy")),
            P(None, ("gx", "gy")),
            P(("gx", "gy")),
        ),
        out_specs=(P(None, "gx", "gy"), P(None, ("gx", "gy")), P(None, ("gx", "gy"))),
        check_vma=False,
    )
```

```python
import math

import jax
import jax.numpy as jnp
import numpy as np
from jax import lax
from jax.experimental import pallas as pl
from jax.experimental.pallas import tpu as pltpu
from jax.sharding import PartitionSpec as P

ROWB = 128
PSIZE = 128
STEN = 4
EDGE = 32
ROWS = 192
CHUNK = 64
EXTRA = 2
HALO = 8
R_DECAY = (3.0 - math.sqrt(5.0)) / 2.0
F32 = jnp.float32
BF16 = jnp.bfloat16


def kernel_taps(reach):
    level = 3.0 / math.sqrt(5.0)

    def inverse(n):
        return level * (-R_DECAY) ** abs(n)

    taps = np.zeros(reach + 1)
    for n in range(reach + 1):
        taps[n] = (7.0 / 9.0) * (inverse(n + 1) - inverse(n - 1)) + (1.0 / 36.0) * (
            inverse(n + 2) - inverse(n - 2)
        )
    return taps


TAPS = kernel_taps(600)
TAIL = TAPS[2] / R_DECAY**2
FIRST = TAPS[1] + TAIL * R_DECAY


def split(values, terms):
    parts = []
    for _ in range(terms):
        part = values.astype(BF16)
        parts.append(part)
        values = values - part.astype(F32)
    return parts


def toeplitz(offset, rows, window):
    distance = offset + np.arange(rows)[:, None] - np.arange(window)[None, :]
    full = np.sign(distance) * TAPS[np.abs(distance)]
    high = full.astype(BF16)
    low = (full - high.astype(np.float64)).astype(BF16)
    return np.stack([high, low])


def edge_state(rows, from_first):
    index = lax.broadcasted_iota(jnp.int32, rows.shape, 0)
    steps = index + 1 if from_first else EDGE - index
    parity = 1.0 - 2.0 * (steps & 1).astype(F32)
    decay = parity * jnp.exp(steps.astype(F32) * math.log(R_DECAY))
    return jnp.sum(rows * decay, 0, keepdims=True)


def prep_body(x_cells, live, head, tail, cells, weights, offsets, to_right, to_left, request):
    zero = jnp.zeros((to_left.shape[0] - 6, head.shape[2]), F32)
    to_left[...] = jnp.concatenate(
        [edge_state(head[c], True) for c in range(3)] + [head[c, 0:1, :] for c in range(3)] + [zero], 0
    )
    to_right[...] = jnp.concatenate(
        [edge_state(tail[c], False) for c in range(3)]
        + [tail[c, EDGE - 1 : EDGE, :] for c in range(3)]
        + [zero],
        0,
    )
    cell = cells[...]
    slots = cell.shape[1]
    row = jnp.floor((cell.astype(F32) + 0.5) * (1.0 / x_cells)).astype(jnp.int32)
    x = cell - row * x_cells
    line = row & (ROWB - 1)
    slot = (row >> 7)[0:1]
    lane = lax.broadcasted_iota(jnp.int32, (1, slots), 1)
    limit = jnp.zeros((1, slots), jnp.int32)
    for k in range(slots // PSIZE):
        limit = jnp.where(lane // PSIZE == k, live[k], limit)
    alive = lane % PSIZE < limit
    key = jnp.where(alive, slot, -1).astype(F32)
    w_high, w_low = split(weights[...], 2)
    o_high, o_low = split(offsets[...].reshape(1, slots), 2)
    request[...] = jnp.concatenate(
        [
            (x >> 3).astype(F32),
            (x & 7).astype(F32),
            line.astype(F32),
            w_high.astype(F32),
            w_low.astype(F32),
            o_high.astype(F32),
            o_low.astype(F32),
            key,
            jnp.zeros((9, slots), F32),
        ],
        0,
    ).astype(BF16)


def table_body(plan, v_ref, t_ref, table_ref):
    window, columns = t_ref.shape[1:]
    x_cells, lines = v_ref.shape[1:]
    blocks = lines // ROWB
    width = 3 * ROWB
    for c in range(3):
        turned = [
            jnp.transpose(v_ref[c, :, b * ROWB : (b + 1) * ROWB].astype(BF16))
            for b in range(blocks)
        ]
        for b in range(blocks):
            table_ref[b, c * ROWB : (c + 1) * ROWB] = turned[b]
        turned = jnp.concatenate(turned, 0)
        for column, start, kind in plan:
            out = jnp.dot(
                turned[:, start : start + window], t_ref[kind], preferred_element_type=F32
            ).astype(BF16)
            for b in range(blocks):
                table_ref[
                    b, width + c * ROWB : width + (c + 1) * ROWB, column : column + columns
                ] = out[b * ROWB : (b + 1) * ROWB]


def derivative_body(plan, v_ref, t_ref, left_ref, right_ref, after_ref, g_ref, out_buf, sems):
    del after_ref
    window = t_ref.shape[3]
    x_cells = v_ref.shape[1]
    parts = [split(v_ref[c], 2) for c in range(3)]
    copies = []
    for number, (row, start, kind) in enumerate(plan):
        t_high, t_low = t_ref[kind, 0], t_ref[kind, 1]
        for c in range(3):
            high = parts[c][0][start : start + window]
            low = parts[c][1][start : start + window]
            out = (
                jnp.dot(t_high, high, preferred_element_type=F32)
                + jnp.dot(t_high, low, preferred_element_type=F32)
                + jnp.dot(t_low, high, preferred_element_type=F32)
            )
            out_buf[c, row : row + ROWS] = out
            if row == 0:
                out_buf[c, :EDGE] = edge_fix(
                    out[:EDGE], left_ref[c : c + 1], left_ref[c + 3 : c + 4], True
                )
            if row + ROWS == x_cells:
                out_buf[c, x_cells - EDGE :] = edge_fix(
                    out_buf[c, x_cells - EDGE :],
                    right_ref[c : c + 1],
                    right_ref[c + 3 : c + 4],
                    False,
                )
        copy = pltpu.make_async_copy(
            out_buf.at[:, pl.ds(row, ROWS)], g_ref.at[:, pl.ds(row, ROWS)], sems.at[number]
        )
        copy.start()
        copies.append(copy)
    for copy in copies:
        copy.wait()


def edge_fix(rows, state, plane, is_left):
    index = lax.broadcasted_iota(jnp.int32, rows.shape, 0)
    steps = index if is_left else EDGE - 1 - index
    parity = 1.0 - 2.0 * (steps & 1).astype(F32)
    decay = parity * jnp.exp(steps.astype(F32) * math.log(R_DECAY))
    sign = 1.0 if is_left else -1.0
    return rows + (sign * TAIL) * decay * state + jnp.where(steps == 0, sign * FIRST, 0.0) * plane


def signed_decay(steps):
    parity = 1.0 - 2.0 * (steps.astype(jnp.int32) & 1).astype(F32)
    return parity * jnp.exp(steps * math.log(R_DECAY))


def lookup_body(owners, xor, owner_ref, table_ref, left_ref, right_ref, *refs):
    request_refs = refs[:owners]
    out_refs = refs[owners : 2 * owners]
    requests, ranks, totals, states, peer_at = refs[2 * owners :]
    blocks, _, x_cells = table_ref.shape
    width = 3 * ROWB
    me = lax.axis_index("gy")
    capacity = blocks // 2
    slots = requests.shape[2]
    groups = slots // ROWB
    cells = STEN * CHUNK

    peers = []
    for block in range(blocks):
        owner = owner_ref[0, me * blocks + block]
        peers.append((owner ^ me) if xor else lax.rem(owner - me + owners, owners))
        peer_at[block] = peers[block]
    for k in range(owners):
        requests[k] = request_refs[k][...]
        totals[k] = jnp.zeros(totals.shape[1:], F32)
    for block in range(blocks):
        at = slice(block * ROWB, (block + 1) * ROWB)
        states[block] = jnp.transpose(
            jnp.concatenate([left_ref[:8, at], right_ref[:8, at]], 0)
        ).astype(BF16)

    matched = []
    for block in range(blocks):
        rank = jnp.int32(0)
        for earlier in range(block):
            rank += (peers[earlier] == peers[block]).astype(jnp.int32)
        key = requests[peers[block], 16:32, :].astype(F32)[6:7]
        matched.append(jnp.where(key == (me * capacity + rank).astype(F32), 1.0, 0.0))
    stacked = jnp.concatenate(
        [m[:, k * ROWB : (k + 1) * ROWB] for m in matched for k in range(groups)], 0
    )
    upto = lax.broadcasted_iota(jnp.int32, (ROWB, ROWB), 0) <= lax.broadcasted_iota(
        jnp.int32, (ROWB, ROWB), 1
    )
    running = jnp.dot(
        stacked.astype(BF16), jnp.where(upto, 1.0, 0.0).astype(BF16), preferred_element_type=F32
    )
    ends = []
    end = jnp.int32(0)
    for block in range(blocks):
        before = jnp.zeros((1, 1), F32)
        pieces = []
        for k in range(groups):
            r = block * groups + k
            line = running[r : r + 1]
            pieces.append(jnp.where(stacked[r : r + 1] > 0.5, line - 1.0 + before, -1.0))
            before = before + line[:, ROWB - 1 : ROWB]
        ranks[block] = jnp.concatenate(pieces, 1)
        count = before[0, 0].astype(jnp.int32)
        end = end + jnp.maximum((count + CHUNK - 1) // CHUNK - 1, 0)
        ends.append(end)

    x_iota = lax.broadcasted_iota(jnp.int32, (x_cells, cells), 0).astype(F32)
    line_iota = lax.broadcasted_iota(jnp.int32, (ROWB, cells), 0).astype(F32)
    state_iota = lax.broadcasted_iota(jnp.int32, (16, cells), 0)
    place = lax.broadcasted_iota(jnp.int32, (CHUNK, slots), 0)
    low_half = lax.broadcasted_iota(jnp.int32, (1, 2 * CHUNK), 1) < CHUNK

    def batch(tasks):
        chosen, data = [], []
        for block, peer, i in tasks:
            one = jnp.where(ranks[block] == (place + i * CHUNK).astype(F32), 1.0, 0.0).astype(BF16)
            chosen.append(jnp.concatenate([one, one], 0))
        for (block, peer, i), pick in zip(tasks, chosen):
            data.append(
                lax.dot_general(
                    requests[peer], pick, (((1,), (1,)), ((), ())), preferred_element_type=F32
                )
            )
        found, halos, masks, offsets = [], [], [], []
        for (block, peer, i), d in zip(tasks, data):

            def by_cell(row):
                pairs = [
                    jnp.where(low_half, d[row + s : row + s + 1], d[row + s + 1 : row + s + 2])
                    for s in (0, 2)
                ]
                return jnp.concatenate(pairs, 1)

            x = by_cell(0) * 8.0 + by_cell(4)
            weight = by_cell(12) + by_cell(16)
            offset = d[20:21] + d[21:22]
            offsets.append(jnp.concatenate([offset, offset], 1))
            masks.append(jnp.where(line_iota == by_cell(8), weight, 0.0))
            pick = jnp.where(x_iota == x, 1.0, 0.0).astype(BF16)
            found.append(jnp.dot(table_ref[block], pick, preferred_element_type=F32))
            y = x_cells - 1.0 - x
            left = jnp.where(x < EDGE, TAIL * signed_decay(x), 0.0)
            right = jnp.where(y < EDGE, -TAIL * signed_decay(y), 0.0)
            left_first = jnp.where(x == 0.0, FIRST, 0.0)
            right_first = jnp.where(y == 0.0, -FIRST, 0.0)
            terms = []
            for c in range(3):
                term = jnp.where(state_iota == c, left, 0.0)
                term = jnp.where(state_iota == c + 3, left_first, term)
                term = jnp.where(state_iota == c + 8, right, term)
                terms.append(jnp.where(state_iota == c + 11, right_first, term))
            halos.append(
                jnp.dot(
                    states[block],
                    jnp.concatenate(terms, 1).astype(BF16),
                    preferred_element_type=F32,
                )
            )
        for (block, peer, i), f, h, mask, offset, pick in zip(
            tasks, found, halos, masks, offsets, chosen
        ):
            sums = []
            for c in range(3):
                carried = f[c * ROWB : (c + 1) * ROWB]
                slope = f[width + c * ROWB : width + (c + 1) * ROWB]
                slope = slope + h[:, c * cells : (c + 1) * cells]
                sums.append(jnp.sum((carried + offset * slope) * mask, 0, keepdims=True))
            sums.append(jnp.zeros((1, cells), F32))
            value = jnp.concatenate(sums, 0)
            value = value[:, : 2 * CHUNK] + value[:, 2 * CHUNK :]
            back = jnp.concatenate(
                [p.astype(F32) for p in split(value, 3)] + [jnp.zeros((4, 2 * CHUNK), F32)], 0
            )
            totals[peer] += jnp.dot(back.astype(BF16), pick, preferred_element_type=F32)

    batch([(block, peers[block], jnp.int32(0)) for block in range(blocks)])

    def extra(number):
        block = jnp.int32(0)
        first = jnp.int32(0)
        for b in range(blocks - 1):
            past = number >= ends[b]
            block = jnp.where(past, b + 1, block)
            first = jnp.where(past, ends[b], first)
        return block, peer_at[block], number - first + 1

    @pl.loop(0, (ends[-1] + EXTRA - 1) // EXTRA)
    def _(i):
        batch([extra(i * EXTRA + t) for t in range(EXTRA)])

    for k in range(owners):
        total = totals[k]
        out_refs[k][...] = total[0:8] + pltpu.roll(total[0:8], 4, 0) + total[8:16]


def final_body(live, relax, particle, *refs):
    parts, (fluid_ref, updated_ref) = refs[:-2], refs[-2:]
    raw = parts[0][0:3]
    for part in parts[1:]:
        raw = raw + part[0:3]
    slots = raw.shape[1]
    lane = lax.broadcasted_iota(jnp.int32, (3, slots), 1)
    limit = jnp.zeros((3, slots), jnp.int32)
    for k in range(slots // PSIZE):
        limit = jnp.where(lane // PSIZE == k, live[k], limit)
    alive = lane % PSIZE < limit
    fluid = jnp.where(alive, raw, 0.0)
    velocity = particle[...]
    fluid_ref[...] = fluid
    updated_ref[...] = jnp.where(
        alive, velocity + relax[...].reshape(1, slots) * (fluid - velocity), velocity
    )


def sent(values, axis, pairs):
    return lax.ppermute(values, axis, pairs)


def per_device(
    velocity, row_owner, cell_list, weights, offsets, relax_rate, particle_velocity, live_counts
):
    components, x_cells, lines = velocity.shape
    slots = weights.shape[1]
    columns = lax.axis_size("gx")
    owners = lax.axis_size("gy")
    blocks = lines // ROWB
    xor = owners & (owners - 1) == 0
    vmem = pl.BlockSpec(memory_space=pltpu.VMEM)
    smem = pl.BlockSpec(memory_space=pltpu.SMEM)
    hbm = pl.BlockSpec(memory_space=pltpu.HBM)
    limit = 24 * 1024 * 1024
    one = lambda shape: pl.BlockSpec(shape, lambda i: (0,) * len(shape))

    last = x_cells // EDGE - 1
    to_right, to_left, request = pl.pallas_call(
        lambda *refs: prep_body(x_cells, *refs),
        grid=(1,),
        in_specs=[
            smem,
            pl.BlockSpec((3, EDGE, lines), lambda i: (0, 0, 0)),
            pl.BlockSpec((3, EDGE, lines), lambda i: (0, last, 0)),
            one((STEN, slots)),
            one((STEN, slots)),
            one((slots,)),
        ],
        out_specs=[vmem] * 3,
        out_shape=[
            jax.ShapeDtypeStruct((HALO, lines), F32),
            jax.ShapeDtypeStruct((HALO, lines), F32),
            jax.ShapeDtypeStruct((32, slots), BF16),
        ],
        name="prepare",
    )(live_counts, velocity, velocity, cell_list, weights, offsets)

    from_left = sent(to_right, "gx", [(i, (i + 1) % columns) for i in range(columns)])
    from_right = sent(to_left, "gx", [((i + 1) % columns, i) for i in range(columns)])

    def peer(i, k):
        return i ^ k if xor else (i + k) % owners

    requests = [request] + [
        sent(request, "gy", [(peer(i, k), i) for i in range(owners)]) for k in range(1, owners)
    ]

    window = min(256, x_cells)
    plan, kinds = [], []
    for row in range(0, x_cells, ROWS):
        start = min(max(row - EDGE, 0), x_cells - window)
        if row - start not in kinds:
            kinds.append(row - start)
        plan.append((row, start, kinds.index(row - start)))
    matrices = jnp.asarray(np.stack([toeplitz(o, ROWS, window) for o in kinds]))
    width = 3 * ROWB
    columns_at = 256 if x_cells % 256 == 0 else x_cells
    reach = min(512, x_cells)
    across, across_kinds = [], []
    for column in range(0, x_cells, columns_at):
        start = min(max(column - ROWB, 0), x_cells - reach)
        if column - start not in across_kinds:
            across_kinds.append(column - start)
        across.append((column, start, across_kinds.index(column - start)))
    turned = jnp.asarray(np.stack([toeplitz(o, columns_at, reach)[0].T for o in across_kinds]))
    table = pl.pallas_call(
        lambda *refs: table_body(across, *refs),
        in_specs=[vmem, vmem],
        out_specs=vmem,
        out_shape=jax.ShapeDtypeStruct((blocks, 2 * width, x_cells), BF16),
        compiler_params=pltpu.CompilerParams(vmem_limit_bytes=limit),
        cost_estimate=pl.CostEstimate(
            flops=2 * window * velocity.size, bytes_accessed=8 * velocity.size, transcendentals=0
        ),
        name="table",
    )(velocity, turned)

    partials = pl.pallas_call(
        lambda *refs: lookup_body(owners, xor, *refs),
        in_specs=[smem] + [vmem] * (3 + owners),
        out_specs=[vmem] * owners,
        out_shape=[jax.ShapeDtypeStruct((8, slots), F32)] * owners,
        scratch_shapes=[
            pltpu.VMEM((owners, 32, slots), BF16),
            pltpu.VMEM((blocks, 1, slots), F32),
            pltpu.VMEM((owners, 16, slots), F32),
            pltpu.VMEM((blocks, ROWB, 16), BF16),
            pltpu.SMEM((blocks,), jnp.int32),
        ],
        compiler_params=pltpu.CompilerParams(vmem_limit_bytes=limit),
        cost_estimate=pl.CostEstimate(
            flops=2 * 768 * 6 * x_cells * 1024, bytes_accessed=2 * velocity.size, transcendentals=0
        ),
        name="lookup",
    )(row_owner, table, from_left, from_right, *requests)

    gradient = pl.pallas_call(
        lambda *refs: derivative_body(plan, *refs),
        in_specs=[vmem] * 5,
        out_specs=hbm,
        out_shape=jax.ShapeDtypeStruct(velocity.shape, F32),
        scratch_shapes=[
            pltpu.VMEM(velocity.shape, F32),
            pltpu.SemaphoreType.DMA((len(plan),)),
        ],
        compiler_params=pltpu.CompilerParams(vmem_limit_bytes=limit),
        cost_estimate=pl.CostEstimate(
            flops=6 * window * velocity.size, bytes_accessed=8 * velocity.size, transcendentals=0
        ),
        name="derivative",
    )(velocity, matrices, from_left, from_right, partials[0])

    returned = [partials[0]] + [
        sent(partials[k], "gy", [(i, peer(i, k)) for i in range(owners)]) for k in range(1, owners)
    ]
    shape = jax.ShapeDtypeStruct((3, slots), F32)
    fluid, updated = pl.pallas_call(
        final_body,
        in_specs=[smem] + [vmem] * (2 + owners),
        out_specs=[vmem] * 2,
        out_shape=[shape, shape],
        compiler_params=pltpu.CompilerParams(vmem_limit_bytes=limit),
        name="finish",
    )(live_counts, relax_rate, particle_velocity, *returned)
    return (gradient, fluid, updated)


def solution(mesh):
    return jax.shard_map(
        per_device,
        mesh=mesh,
        in_specs=(
            P(None, "gx", "gy"),
            P("gx", None),
            P(None, ("gx", "gy")),
            P(None, ("gx", "gy")),
            P(("gx", "gy")),
            P(("gx", "gy")),
            P(None, ("gx", "gy")),
            P(("gx", "gy")),
        ),
        out_specs=(P(None, "gx", "gy"), P(None, ("gx", "gy")), P(None, ("gx", "gy"))),
        check_vma=False,
    )
```

```python
import math

import jax
import jax.numpy as jnp
import numpy as np
from jax import lax
from jax.experimental import pallas as pl
from jax.experimental.pallas import tpu as pltpu
from jax.sharding import PartitionSpec as P

ROWB = 128
PSIZE = 128
STEN = 4
EDGE = 32
ROWS = 192
CHUNK = 64
EXTRA = 2
LOAD = 43
R_DECAY = (3.0 - math.sqrt(5.0)) / 2.0
F32 = jnp.float32
BF16 = jnp.bfloat16


def kernel_taps(reach):
    level = 3.0 / math.sqrt(5.0)

    def inverse(n):
        return level * (-R_DECAY) ** abs(n)

    taps = np.zeros(reach + 1)
    for n in range(reach + 1):
        taps[n] = (7.0 / 9.0) * (inverse(n + 1) - inverse(n - 1)) + (1.0 / 36.0) * (
            inverse(n + 2) - inverse(n - 2)
        )
    return taps


TAPS = kernel_taps(600)
TAIL = TAPS[2] / R_DECAY**2
FIRST = TAPS[1] + TAIL * R_DECAY


def split(values, terms):
    parts = []
    for _ in range(terms):
        part = values.astype(BF16)
        parts.append(part)
        values = values - part.astype(F32)
    return parts


def toeplitz(offset, rows, window):
    distance = offset + np.arange(rows)[:, None] - np.arange(window)[None, :]
    full = np.sign(distance) * TAPS[np.abs(distance)]
    high = full.astype(BF16)
    low = (full - high.astype(np.float64)).astype(BF16)
    return np.stack([high, low])


def edge_state(rows, from_first):
    index = lax.broadcasted_iota(jnp.int32, rows.shape, 0)
    steps = index + 1 if from_first else EDGE - index
    parity = 1.0 - 2.0 * (steps & 1).astype(F32)
    decay = parity * jnp.exp(steps.astype(F32) * math.log(R_DECAY))
    return jnp.sum(rows * decay, 0, keepdims=True)


def even_column():
    return lax.rem(lax.axis_index("gx"), 2) == 0


def neighbours(chip_ref, next_ref):
    is_even = even_column()
    chip, following = chip_ref[...], next_ref[...]
    return jnp.where(is_even, following, chip), jnp.where(is_even, chip, following)


def prep_body(x_cells, live, head, tail, cells, weights, offsets, request, to_chip, to_next):
    zero = jnp.zeros((2, head.shape[2]), F32)
    to_left = jnp.concatenate(
        [edge_state(head[c], True) for c in range(3)] + [head[c, 0:1, :] for c in range(3)] + [zero], 0
    )
    to_right = jnp.concatenate(
        [edge_state(tail[c], False) for c in range(3)]
        + [tail[c, EDGE - 1 : EDGE, :] for c in range(3)]
        + [zero],
        0,
    )
    is_even = even_column()
    to_chip[...] = jnp.where(is_even, to_right, to_left)
    to_next[...] = jnp.where(is_even, to_left, to_right)
    cell = cells[...]
    slots = cell.shape[1]
    row = jnp.floor((cell.astype(F32) + 0.5) * (1.0 / x_cells)).astype(jnp.int32)
    x = cell - row * x_cells
    line = row & (ROWB - 1)
    slot = (row >> 7)[0:1]
    lane = lax.broadcasted_iota(jnp.int32, (1, slots), 1)
    limit = jnp.zeros((1, slots), jnp.int32)
    for k in range(slots // PSIZE):
        limit = jnp.where(lane // PSIZE == k, live[k], limit)
    alive = lane % PSIZE < limit
    key = jnp.where(alive, slot, -1).astype(F32)
    w_high, w_low = split(weights[...], 2)
    o_high, o_low = split(offsets[...].reshape(1, slots), 2)
    request[...] = jnp.concatenate(
        [
            (x >> 3).astype(F32),
            (x & 7).astype(F32),
            line.astype(F32),
            w_high.astype(F32),
            w_low.astype(F32),
            o_high.astype(F32),
            o_low.astype(F32),
            key,
            jnp.zeros((9, slots), F32),
        ],
        0,
    ).astype(BF16)


def table_body(plan, v_ref, t_ref, held_ref, table_ref, sems):
    window, columns = t_ref.shape[1:]
    x_cells, lines = v_ref.shape[1:]
    blocks = lines // ROWB
    width = 3 * ROWB
    parts = 1
    each = blocks // parts
    pieces = [(c, p) for c in range(3) for p in range(parts)]
    copies = []
    for k, (c, p) in enumerate(pieces):
        here = (c, slice(None), pl.ds(p * each * ROWB, each * ROWB))
        copies.append(pltpu.make_async_copy(v_ref.at[here], held_ref.at[here], sems.at[k]))
        copies[-1].start()
    for copy, (c, p) in zip(copies, pieces):
        copy.wait()
        mine = range(p * each, (p + 1) * each)
        turned = [
            jnp.transpose(held_ref[c, :, b * ROWB : (b + 1) * ROWB].astype(BF16)) for b in mine
        ]
        for b, rows in zip(mine, turned):
            table_ref[b, c * ROWB : (c + 1) * ROWB] = rows
        turned = jnp.concatenate(turned, 0)
        for column, start, kind in plan:
            out = jnp.dot(
                turned[:, start : start + window], t_ref[kind], preferred_element_type=F32
            ).astype(BF16)
            for k, b in enumerate(mine):
                table_ref[
                    b, width + c * ROWB : width + (c + 1) * ROWB, column : column + columns
                ] = out[k * ROWB : (k + 1) * ROWB]


def derivative_body(plan, v_ref, t_ref, sides_ref, g_ref, out_buf, sems):
    left, right = sides_ref[:8], sides_ref[8:]
    window = t_ref.shape[3]
    x_cells = v_ref.shape[1]
    parts = [split(v_ref[c], 2) for c in range(3)]
    copies = []
    for number, (row, start, kind) in enumerate(plan):
        t_high, t_low = t_ref[kind, 0], t_ref[kind, 1]
        for c in range(3):
            high = parts[c][0][start : start + window]
            low = parts[c][1][start : start + window]
            out = (
                jnp.dot(t_high, high, preferred_element_type=F32)
                + jnp.dot(t_high, low, preferred_element_type=F32)
                + jnp.dot(t_low, high, preferred_element_type=F32)
            )
            out_buf[c, row : row + ROWS] = out
            if row == 0:
                out_buf[c, :EDGE] = edge_fix(
                    out[:EDGE], left[c : c + 1], left[c + 3 : c + 4], True
                )
            if row + ROWS == x_cells:
                out_buf[c, x_cells - EDGE :] = edge_fix(
                    out_buf[c, x_cells - EDGE :],
                    right[c : c + 1],
                    right[c + 3 : c + 4],
                    False,
                )
        copy = pltpu.make_async_copy(
            out_buf.at[:, pl.ds(row, ROWS)], g_ref.at[:, pl.ds(row, ROWS)], sems.at[number]
        )
        copy.start()
        copies.append(copy)
    for copy in copies:
        copy.wait()


def edge_fix(rows, state, plane, is_left):
    index = lax.broadcasted_iota(jnp.int32, rows.shape, 0)
    steps = index if is_left else EDGE - 1 - index
    parity = 1.0 - 2.0 * (steps & 1).astype(F32)
    decay = parity * jnp.exp(steps.astype(F32) * math.log(R_DECAY))
    sign = 1.0 if is_left else -1.0
    return rows + (sign * TAIL) * decay * state + jnp.where(steps == 0, sign * FIRST, 0.0) * plane


def signed_decay(steps):
    parity = 1.0 - 2.0 * (steps.astype(jnp.int32) & 1).astype(F32)
    return parity * jnp.exp(steps * math.log(R_DECAY))


def lookup_body(owners, xor, owner_ref, next_ref, chip_ref, table_ref, *refs):
    request_refs = refs[:owners]
    out_refs = refs[owners : 2 * owners]
    sides_ref = refs[2 * owners]
    requests, ranks, totals, states, peer_at = refs[2 * owners + 1 :]
    blocks, _, x_cells = table_ref.shape
    width = 3 * ROWB
    me = lax.axis_index("gy")
    capacity = blocks // 2
    slots = requests.shape[2]
    groups = slots // ROWB
    cells = STEN * CHUNK

    peers = []
    for block in range(blocks):
        owner = owner_ref[0, me * blocks + block]
        peers.append((owner ^ me) if xor else lax.rem(owner - me + owners, owners))
        peer_at[block] = peers[block]
    for k in range(owners):
        requests[k] = request_refs[k][...]
        totals[k] = jnp.zeros(totals.shape[1:], F32)
    sides = jnp.concatenate(neighbours(chip_ref, next_ref), 0)
    sides_ref[...] = sides
    for block in range(blocks):
        states[block] = jnp.transpose(sides[:, block * ROWB : (block + 1) * ROWB]).astype(BF16)

    matched = []
    for block in range(blocks):
        rank = jnp.int32(0)
        for earlier in range(block):
            rank += (peers[earlier] == peers[block]).astype(jnp.int32)
        key = requests[peers[block], 16:32, :].astype(F32)[6:7]
        matched.append(jnp.where(key == (me * capacity + rank).astype(F32), 1.0, 0.0))
    stacked = jnp.concatenate(
        [m[:, k * ROWB : (k + 1) * ROWB] for m in matched for k in range(groups)], 0
    )
    upto = lax.broadcasted_iota(jnp.int32, (ROWB, ROWB), 0) <= lax.broadcasted_iota(
        jnp.int32, (ROWB, ROWB), 1
    )
    running = jnp.dot(
        stacked.astype(BF16), jnp.where(upto, 1.0, 0.0).astype(BF16), preferred_element_type=F32
    )
    ends = []
    end = jnp.int32(0)
    for block in range(blocks):
        before = jnp.zeros((1, 1), F32)
        pieces = []
        for k in range(groups):
            r = block * groups + k
            line = running[r : r + 1]
            pieces.append(jnp.where(stacked[r : r + 1] > 0.5, line - 1.0 + before, -1.0))
            before = before + line[:, ROWB - 1 : ROWB]
        ranks[block] = jnp.concatenate(pieces, 1)
        count = before[0, 0].astype(jnp.int32)
        end = end + jnp.maximum((count + CHUNK - 1) // CHUNK - 1, 0)
        ends.append(end)

    x_iota = lax.broadcasted_iota(jnp.int32, (x_cells, cells), 0).astype(F32)
    line_iota = lax.broadcasted_iota(jnp.int32, (ROWB, cells), 0).astype(F32)
    state_iota = lax.broadcasted_iota(jnp.int32, (16, cells), 0)
    place = lax.broadcasted_iota(jnp.int32, (CHUNK, slots), 0)
    low_half = lax.broadcasted_iota(jnp.int32, (1, 2 * CHUNK), 1) < CHUNK

    def batch(tasks):
        chosen, data = [], []
        for block, peer, i in tasks:
            one = jnp.where(ranks[block] == (place + i * CHUNK).astype(F32), 1.0, 0.0).astype(BF16)
            chosen.append(jnp.concatenate([one, one], 0))
        for (block, peer, i), pick in zip(tasks, chosen):
            data.append(
                lax.dot_general(
                    requests[peer], pick, (((1,), (1,)), ((), ())), preferred_element_type=F32
                )
            )
        found, halos, masks, offsets = [], [], [], []
        for (block, peer, i), d in zip(tasks, data):

            def by_cell(row):
                pairs = [
                    jnp.where(low_half, d[row + s : row + s + 1], d[row + s + 1 : row + s + 2])
                    for s in (0, 2)
                ]
                return jnp.concatenate(pairs, 1)

            x = by_cell(0) * 8.0 + by_cell(4)
            weight = by_cell(12) + by_cell(16)
            offset = d[20:21] + d[21:22]
            offsets.append(jnp.concatenate([offset, offset], 1))
            masks.append(jnp.where(line_iota == by_cell(8), weight, 0.0))
            pick = jnp.where(x_iota == x, 1.0, 0.0).astype(BF16)
            found.append(jnp.dot(table_ref[block], pick, preferred_element_type=F32))
            y = x_cells - 1.0 - x
            left = jnp.where(x < EDGE, TAIL * signed_decay(x), 0.0)
            right = jnp.where(y < EDGE, -TAIL * signed_decay(y), 0.0)
            left_first = jnp.where(x == 0.0, FIRST, 0.0)
            right_first = jnp.where(y == 0.0, -FIRST, 0.0)
            terms = []
            for c in range(3):
                term = jnp.where(state_iota == c, left, 0.0)
                term = jnp.where(state_iota == c + 3, left_first, term)
                term = jnp.where(state_iota == c + 8, right, term)
                terms.append(jnp.where(state_iota == c + 11, right_first, term))
            halos.append(
                jnp.dot(
                    states[block],
                    jnp.concatenate(terms, 1).astype(BF16),
                    preferred_element_type=F32,
                )
            )
        for (block, peer, i), f, h, mask, offset, pick in zip(
            tasks, found, halos, masks, offsets, chosen
        ):
            sums = []
            for c in range(3):
                carried = f[c * ROWB : (c + 1) * ROWB]
                slope = f[width + c * ROWB : width + (c + 1) * ROWB]
                slope = slope + h[:, c * cells : (c + 1) * cells]
                sums.append(jnp.sum((carried + offset * slope) * mask, 0, keepdims=True))
            sums.append(jnp.zeros((1, cells), F32))
            value = jnp.concatenate(sums, 0)
            value = value[:, : 2 * CHUNK] + value[:, 2 * CHUNK :]
            back = jnp.concatenate(
                [p.astype(F32) for p in split(value, 3)] + [jnp.zeros((4, 2 * CHUNK), F32)], 0
            )
            totals[peer] += jnp.dot(back.astype(BF16), pick, preferred_element_type=F32)

    batch([(block, peers[block], jnp.int32(0)) for block in range(blocks)])

    def extra(number):
        block = jnp.int32(0)
        first = jnp.int32(0)
        for b in range(blocks - 1):
            past = number >= ends[b]
            block = jnp.where(past, b + 1, block)
            first = jnp.where(past, ends[b], first)
        return block, peer_at[block], number - first + 1

    @pl.loop(0, (ends[-1] + EXTRA - 1) // EXTRA)
    def _(i):
        batch([extra(i * EXTRA + t) for t in range(EXTRA)])

    for k in range(owners):
        total = totals[k]
        out_refs[k][...] = total[0:8] + pltpu.roll(total[0:8], 4, 0) + total[8:16]


def final_body(live, relax, particle, *refs):
    parts, (fluid_ref, updated_ref) = refs[:-2], refs[-2:]
    raw = parts[0][0:3]
    for part in parts[1:]:
        raw = raw + part[0:3]
    slots = raw.shape[1]
    lane = lax.broadcasted_iota(jnp.int32, (3, slots), 1)
    limit = jnp.zeros((3, slots), jnp.int32)
    for k in range(slots // PSIZE):
        limit = jnp.where(lane // PSIZE == k, live[k], limit)
    alive = lane % PSIZE < limit
    fluid = jnp.where(alive, raw, 0.0)
    velocity = particle[...]
    fluid_ref[...] = fluid
    updated_ref[...] = jnp.where(
        alive, velocity + relax[...].reshape(1, slots) * (fluid - velocity), velocity
    )


def sent(values, axis, pairs):
    return lax.ppermute(values, axis, pairs)


def per_device(
    velocity, row_owner, cell_list, weights, offsets, relax_rate, particle_velocity, live_counts
):
    components, x_cells, lines = velocity.shape
    slots = weights.shape[1]
    columns = lax.axis_size("gx")
    owners = lax.axis_size("gy")
    blocks = lines // ROWB
    xor = owners & (owners - 1) == 0
    vmem = pl.BlockSpec(memory_space=pltpu.VMEM)
    smem = pl.BlockSpec(memory_space=pltpu.SMEM)
    hbm = pl.BlockSpec(memory_space=pltpu.HBM)
    limit = 24 * 1024 * 1024
    one = lambda shape: pl.BlockSpec(shape, lambda i: (0,) * len(shape))

    last = x_cells // EDGE - 1
    request, to_chip, to_next = pl.pallas_call(
        lambda *refs: prep_body(x_cells, *refs),
        grid=(1,),
        in_specs=[
            smem,
            pl.BlockSpec((3, EDGE, lines), lambda i: (0, 0, 0)),
            pl.BlockSpec((3, EDGE, lines), lambda i: (0, last, 0)),
            one((STEN, slots)),
            one((STEN, slots)),
            one((slots,)),
        ],
        out_specs=[vmem] * 3,
        out_shape=[
            jax.ShapeDtypeStruct((32, slots), BF16),
            jax.ShapeDtypeStruct((8, lines), F32),
            jax.ShapeDtypeStruct((8, lines), F32),
        ],
        name="prepare",
    )(live_counts, velocity, velocity, cell_list, weights, offsets)

    after = [(i + 1) % columns if i % 2 else (i - 1) % columns for i in range(columns)]
    from_next = sent(to_next, "gx", [(i, after[i]) for i in range(columns)])
    from_chip = sent(to_chip, "gx", [(i, i ^ 1) for i in range(columns)])

    def peer(i, k):
        return i ^ k if xor else (i + k) % owners

    requests = [request] + [
        sent(request, "gy", [(peer(i, k), i) for i in range(owners)]) for k in range(1, owners)
    ]

    window = min(256, x_cells)
    plan, kinds = [], []
    for row in range(0, x_cells, ROWS):
        start = min(max(row - EDGE, 0), x_cells - window)
        if row - start not in kinds:
            kinds.append(row - start)
        plan.append((row, start, kinds.index(row - start)))
    matrices = jnp.asarray(np.stack([toeplitz(o, ROWS, window) for o in kinds]))
    width = 3 * ROWB
    columns_at = 256 if x_cells % 256 == 0 else x_cells
    reach = min(512, x_cells)
    across, across_kinds = [], []
    for column in range(0, x_cells, columns_at):
        start = min(max(column - ROWB, 0), x_cells - reach)
        if column - start not in across_kinds:
            across_kinds.append(column - start)
        across.append((column, start, across_kinds.index(column - start)))
    turned = jnp.asarray(np.stack([toeplitz(o, columns_at, reach)[0].T for o in across_kinds]))
    held, table = pl.pallas_call(
        lambda *refs: table_body(across, *refs),
        in_specs=[hbm, vmem],
        out_specs=[vmem, vmem],
        out_shape=[
            jax.ShapeDtypeStruct(velocity.shape, F32),
            jax.ShapeDtypeStruct((blocks, 2 * width, x_cells), BF16),
        ],
        scratch_shapes=[pltpu.SemaphoreType.DMA((6,))],
        compiler_params=pltpu.CompilerParams(vmem_limit_bytes=LOAD * 1024 * 1024),
        cost_estimate=pl.CostEstimate(
            flops=2 * window * velocity.size, bytes_accessed=8 * velocity.size, transcendentals=0
        ),
        name="table",
    )(velocity, turned)

    *partials, sides = pl.pallas_call(
        lambda *refs: lookup_body(owners, xor, *refs),
        in_specs=[smem] + [vmem] * (3 + owners),
        out_specs=[vmem] * (owners + 1),
        out_shape=[jax.ShapeDtypeStruct((8, slots), F32)] * owners
        + [jax.ShapeDtypeStruct((16, lines), F32)],
        scratch_shapes=[
            pltpu.VMEM((owners, 32, slots), BF16),
            pltpu.VMEM((blocks, 1, slots), F32),
            pltpu.VMEM((owners, 16, slots), F32),
            pltpu.VMEM((blocks, ROWB, 16), BF16),
            pltpu.SMEM((blocks,), jnp.int32),
        ],
        compiler_params=pltpu.CompilerParams(vmem_limit_bytes=limit),
        cost_estimate=pl.CostEstimate(
            flops=2 * 768 * 6 * x_cells * 1024, bytes_accessed=2 * velocity.size, transcendentals=0
        ),
        name="lookup",
    )(row_owner, from_next, from_chip, table, *requests)

    gradient = pl.pallas_call(
        lambda *refs: derivative_body(plan, *refs),
        in_specs=[vmem] * 3,
        out_specs=hbm,
        out_shape=jax.ShapeDtypeStruct(velocity.shape, F32),
        scratch_shapes=[
            pltpu.VMEM(velocity.shape, F32),
            pltpu.SemaphoreType.DMA((len(plan),)),
        ],
        compiler_params=pltpu.CompilerParams(vmem_limit_bytes=limit),
        cost_estimate=pl.CostEstimate(
            flops=6 * window * velocity.size, bytes_accessed=8 * velocity.size, transcendentals=0
        ),
        name="derivative",
    )(held, matrices, sides)

    returned = [partials[0]] + [
        sent(partials[k], "gy", [(i, peer(i, k)) for i in range(owners)]) for k in range(1, owners)
    ]
    shape = jax.ShapeDtypeStruct((3, slots), F32)
    fluid, updated = pl.pallas_call(
        final_body,
        in_specs=[smem] + [vmem] * (2 + owners),
        out_specs=[vmem] * 2,
        out_shape=[shape, shape],
        compiler_params=pltpu.CompilerParams(vmem_limit_bytes=limit),
        name="finish",
    )(live_counts, relax_rate, particle_velocity, *returned)
    return (gradient, fluid, updated)


def solution(mesh):
    return jax.shard_map(
        per_device,
        mesh=mesh,
        in_specs=(
            P(None, "gx", "gy"),
            P("gx", None),
            P(None, ("gx", "gy")),
            P(None, ("gx", "gy")),
            P(("gx", "gy")),
            P(("gx", "gy")),
            P(None, ("gx", "gy")),
            P(("gx", "gy")),
        ),
        out_specs=(P(None, "gx", "gy"), P(None, ("gx", "gy")), P(None, ("gx", "gy"))),
        check_vma=False,
    )
```

```python
import math

import jax
import jax.numpy as jnp
import numpy as np
from jax import lax
from jax.experimental import pallas as pl
from jax.experimental.pallas import tpu as pltpu
from jax.sharding import PartitionSpec as P

ROWB = 128
PSIZE = 128
STEN = 4
EDGE = 32
ROWS = 192
CHUNK = 64
EXTRA = 2
LOAD = 43
SCALE = 1.95685
R_DECAY = (3.0 - math.sqrt(5.0)) / 2.0
F32 = jnp.float32
BF16 = jnp.bfloat16


def kernel_taps(reach):
    level = 3.0 / math.sqrt(5.0)

    def inverse(n):
        return level * (-R_DECAY) ** abs(n)

    taps = np.zeros(reach + 1)
    for n in range(reach + 1):
        taps[n] = (7.0 / 9.0) * (inverse(n + 1) - inverse(n - 1)) + (1.0 / 36.0) * (
            inverse(n + 2) - inverse(n - 2)
        )
    return taps


TAPS = kernel_taps(600)
TAIL = TAPS[2] / R_DECAY**2
FIRST = TAPS[1] + TAIL * R_DECAY


def split(values, terms):
    parts = []
    for _ in range(terms):
        part = values.astype(BF16)
        parts.append(part)
        values = values - part.astype(F32)
    return parts


def toeplitz(offset, rows, window):
    distance = offset + np.arange(rows)[:, None] - np.arange(window)[None, :]
    return (np.sign(distance) * TAPS[np.abs(distance)] / SCALE).astype(BF16)


def edge_state(rows, from_first):
    index = lax.broadcasted_iota(jnp.int32, rows.shape, 0)
    steps = index + 1 if from_first else EDGE - index
    parity = 1.0 - 2.0 * (steps & 1).astype(F32)
    decay = parity * jnp.exp(steps.astype(F32) * math.log(R_DECAY))
    return jnp.sum(rows * decay, 0, keepdims=True)


def even_column():
    return lax.rem(lax.axis_index("gx"), 2) == 0


def neighbours(chip_ref, next_ref):
    is_even = even_column()
    chip, following = chip_ref[...], next_ref[...]
    return jnp.where(is_even, following, chip), jnp.where(is_even, chip, following)


def prep_body(x_cells, live, head, tail, cells, weights, offsets, request, to_chip, to_next):
    zero = jnp.zeros((2, head.shape[2]), F32)
    to_left = jnp.concatenate(
        [edge_state(head[c], True) for c in range(3)] + [head[c, 0:1, :] for c in range(3)] + [zero], 0
    )
    to_right = jnp.concatenate(
        [edge_state(tail[c], False) for c in range(3)]
        + [tail[c, EDGE - 1 : EDGE, :] for c in range(3)]
        + [zero],
        0,
    )
    is_even = even_column()
    to_chip[...] = jnp.where(is_even, to_right, to_left)
    to_next[...] = jnp.where(is_even, to_left, to_right)
    cell = cells[...]
    slots = cell.shape[1]
    row = jnp.floor((cell.astype(F32) + 0.5) * (1.0 / x_cells)).astype(jnp.int32)
    x = cell - row * x_cells
    line = row & (ROWB - 1)
    slot = (row >> 7)[0:1]
    lane = lax.broadcasted_iota(jnp.int32, (1, slots), 1)
    limit = jnp.zeros((1, slots), jnp.int32)
    for k in range(slots // PSIZE):
        limit = jnp.where(lane // PSIZE == k, live[k], limit)
    alive = lane % PSIZE < limit
    key = jnp.where(alive, slot, -1).astype(F32)
    w_high, w_low = split(weights[...], 2)
    o_high, o_low = split(offsets[...].reshape(1, slots), 2)
    request[...] = jnp.concatenate(
        [
            (x >> 3).astype(F32),
            (x & 7).astype(F32),
            line.astype(F32),
            w_high.astype(F32),
            w_low.astype(F32),
            o_high.astype(F32),
            o_low.astype(F32),
            key,
            jnp.zeros((9, slots), F32),
        ],
        0,
    ).astype(BF16)


def table_body(plan, v_ref, t_ref, held_ref, table_ref, sems):
    window = t_ref.shape[2]
    lines = v_ref.shape[2]
    width = 3 * ROWB
    copies = [pltpu.make_async_copy(v_ref.at[c], held_ref.at[c], sems.at[c]) for c in range(3)]
    for copy in copies:
        copy.start()
    for c in range(3):
        copies[c].wait()
        high = held_ref[c].astype(BF16)
        rows = [
            jnp.dot(t_ref[kind], high[start : start + window], preferred_element_type=F32)
            for row, start, kind in plan
        ]
        slopes = jnp.concatenate([(SCALE * r).astype(BF16) for r in rows], 0)
        for b in range(lines // ROWB):
            at = slice(b * ROWB, (b + 1) * ROWB)
            table_ref[b, c * ROWB : (c + 1) * ROWB] = jnp.transpose(high[:, at])
            table_ref[b, width + c * ROWB : width + (c + 1) * ROWB] = jnp.transpose(slopes[:, at])


def derivative_body(plan, v_ref, t_ref, sides_ref, g_ref, out_buf, sems):
    left, right = sides_ref[:8], sides_ref[8:]
    window = t_ref.shape[2]
    x_cells = v_ref.shape[1]
    copies = []
    for c in range(3):
        high, low = split(v_ref[c], 2)
        sent_to = 0
        for number, (row, start, kind) in enumerate(plan):
            matrix = t_ref[kind]
            both = jnp.concatenate([high[start : start + window], low[start : start + window]], 0)
            out = SCALE * jnp.dot(
                jnp.concatenate([matrix, matrix], 1), both, preferred_element_type=F32
            )
            out_buf[c, row : row + ROWS] = out
            if row == 0:
                out_buf[c, :EDGE] = edge_fix(out[:EDGE], left[c : c + 1], left[c + 3 : c + 4], True)
            if row + ROWS == x_cells:
                out_buf[c, x_cells - EDGE :] = edge_fix(
                    out_buf[c, x_cells - EDGE :], right[c : c + 1], right[c + 3 : c + 4], False
                )
            if number % 2 == 1 or row + ROWS == x_cells:
                rows = pl.ds(sent_to, row + ROWS - sent_to)
                sent_to = row + ROWS
                copy = pltpu.make_async_copy(
                    out_buf.at[c, rows], g_ref.at[c, rows], sems.at[len(copies)]
                )
                copy.start()
                copies.append(copy)
    for copy in copies:
        copy.wait()


def edge_fix(rows, state, plane, is_left):
    index = lax.broadcasted_iota(jnp.int32, rows.shape, 0)
    steps = index if is_left else EDGE - 1 - index
    parity = 1.0 - 2.0 * (steps & 1).astype(F32)
    decay = parity * jnp.exp(steps.astype(F32) * math.log(R_DECAY))
    sign = 1.0 if is_left else -1.0
    return rows + (sign * TAIL) * decay * state + jnp.where(steps == 0, sign * FIRST, 0.0) * plane


def signed_decay(steps):
    parity = 1.0 - 2.0 * (steps.astype(jnp.int32) & 1).astype(F32)
    return parity * jnp.exp(steps * math.log(R_DECAY))


def lookup_body(owners, xor, owner_ref, next_ref, chip_ref, table_ref, *refs):
    request_refs = refs[:owners]
    out_refs = refs[owners : 2 * owners]
    sides_ref = refs[2 * owners]
    requests, ranks, totals, states, peer_at = refs[2 * owners + 1 :]
    blocks, _, x_cells = table_ref.shape
    width = 3 * ROWB
    me = lax.axis_index("gy")
    capacity = blocks // 2
    slots = requests.shape[2]
    groups = slots // ROWB
    cells = STEN * CHUNK

    peers = []
    for block in range(blocks):
        owner = owner_ref[0, me * blocks + block]
        peers.append((owner ^ me) if xor else lax.rem(owner - me + owners, owners))
        peer_at[block] = peers[block]
    for k in range(owners):
        requests[k] = request_refs[k][...]
        totals[k] = jnp.zeros(totals.shape[1:], F32)
    sides = jnp.concatenate(neighbours(chip_ref, next_ref), 0)
    sides_ref[...] = sides
    for block in range(blocks):
        states[block] = jnp.transpose(sides[:, block * ROWB : (block + 1) * ROWB]).astype(BF16)

    matched = []
    for block in range(blocks):
        rank = jnp.int32(0)
        for earlier in range(block):
            rank += (peers[earlier] == peers[block]).astype(jnp.int32)
        key = requests[peers[block], 16:32, :].astype(F32)[6:7]
        matched.append(jnp.where(key == (me * capacity + rank).astype(F32), 1.0, 0.0))
    stacked = jnp.concatenate(
        [m[:, k * ROWB : (k + 1) * ROWB] for m in matched for k in range(groups)], 0
    )
    upto = lax.broadcasted_iota(jnp.int32, (ROWB, ROWB), 0) <= lax.broadcasted_iota(
        jnp.int32, (ROWB, ROWB), 1
    )
    running = jnp.dot(
        stacked.astype(BF16), jnp.where(upto, 1.0, 0.0).astype(BF16), preferred_element_type=F32
    )
    ends = []
    end = jnp.int32(0)
    for block in range(blocks):
        before = jnp.zeros((1, 1), F32)
        pieces = []
        for k in range(groups):
            r = block * groups + k
            line = running[r : r + 1]
            pieces.append(jnp.where(stacked[r : r + 1] > 0.5, line - 1.0 + before, -1.0))
            before = before + line[:, ROWB - 1 : ROWB]
        ranks[block] = jnp.concatenate(pieces, 1)
        count = before[0, 0].astype(jnp.int32)
        end = end + jnp.maximum((count + CHUNK - 1) // CHUNK - 1, 0)
        ends.append(end)

    x_iota = lax.broadcasted_iota(jnp.int32, (x_cells, cells), 0).astype(F32)
    line_iota = lax.broadcasted_iota(jnp.int32, (ROWB, cells), 0).astype(F32)
    state_iota = lax.broadcasted_iota(jnp.int32, (16, cells), 0)
    place = lax.broadcasted_iota(jnp.int32, (CHUNK, slots), 0)
    low_half = lax.broadcasted_iota(jnp.int32, (1, 2 * CHUNK), 1) < CHUNK

    def batch(tasks):
        chosen, data = [], []
        for block, peer, i in tasks:
            one = jnp.where(ranks[block] == (place + i * CHUNK).astype(F32), 1.0, 0.0).astype(BF16)
            chosen.append(jnp.concatenate([one, one], 0))
        for (block, peer, i), pick in zip(tasks, chosen):
            data.append(
                lax.dot_general(
                    requests[peer], pick, (((1,), (1,)), ((), ())), preferred_element_type=F32
                )
            )
        found, halos, masks, offsets = [], [], [], []
        for (block, peer, i), d in zip(tasks, data):

            def by_cell(row):
                pairs = [
                    jnp.where(low_half, d[row + s : row + s + 1], d[row + s + 1 : row + s + 2])
                    for s in (0, 2)
                ]
                return jnp.concatenate(pairs, 1)

            x = by_cell(0) * 8.0 + by_cell(4)
            weight = by_cell(12) + by_cell(16)
            offset = d[20:21] + d[21:22]
            offsets.append(jnp.concatenate([offset, offset], 1))
            masks.append(jnp.where(line_iota == by_cell(8), weight, 0.0))
            pick = jnp.where(x_iota == x, 1.0, 0.0).astype(BF16)
            found.append(jnp.dot(table_ref[block], pick, preferred_element_type=F32))
            y = x_cells - 1.0 - x
            left = jnp.where(x < EDGE, TAIL * signed_decay(x), 0.0)
            right = jnp.where(y < EDGE, -TAIL * signed_decay(y), 0.0)
            left_first = jnp.where(x == 0.0, FIRST, 0.0)
            right_first = jnp.where(y == 0.0, -FIRST, 0.0)
            terms = []
            for c in range(3):
                term = jnp.where(state_iota == c, left, 0.0)
                term = jnp.where(state_iota == c + 3, left_first, term)
                term = jnp.where(state_iota == c + 8, right, term)
                terms.append(jnp.where(state_iota == c + 11, right_first, term))
            halos.append(
                jnp.dot(
                    states[block],
                    jnp.concatenate(terms, 1).astype(BF16),
                    preferred_element_type=F32,
                )
            )
        for (block, peer, i), f, h, mask, offset, pick in zip(
            tasks, found, halos, masks, offsets, chosen
        ):
            sums = []
            for c in range(3):
                carried = f[c * ROWB : (c + 1) * ROWB]
                slope = f[width + c * ROWB : width + (c + 1) * ROWB]
                slope = slope + h[:, c * cells : (c + 1) * cells]
                sums.append(jnp.sum((carried + offset * slope) * mask, 0, keepdims=True))
            sums.append(jnp.zeros((1, cells), F32))
            value = jnp.concatenate(sums, 0)
            value = value[:, : 2 * CHUNK] + value[:, 2 * CHUNK :]
            back = jnp.concatenate(
                [p.astype(F32) for p in split(value, 3)] + [jnp.zeros((4, 2 * CHUNK), F32)], 0
            )
            totals[peer] += jnp.dot(back.astype(BF16), pick, preferred_element_type=F32)

    batch([(block, peers[block], jnp.int32(0)) for block in range(blocks)])

    def extra(number):
        block = jnp.int32(0)
        first = jnp.int32(0)
        for b in range(blocks - 1):
            past = number >= ends[b]
            block = jnp.where(past, b + 1, block)
            first = jnp.where(past, ends[b], first)
        return block, peer_at[block], number - first + 1

    @pl.loop(0, (ends[-1] + EXTRA - 1) // EXTRA)
    def _(i):
        batch([extra(i * EXTRA + t) for t in range(EXTRA)])

    for k in range(owners):
        total = totals[k]
        out_refs[k][...] = total[0:8] + pltpu.roll(total[0:8], 4, 0) + total[8:16]


def final_body(request, relax, particle, *refs):
    parts, (fluid_ref, updated_ref) = refs[:-2], refs[-2:]
    raw = parts[0][0:3]
    for part in parts[1:]:
        raw = raw + part[0:3]
    slots = raw.shape[1]
    alive = jnp.broadcast_to(request[16:32].astype(F32)[6:7], raw.shape) >= 0.0
    fluid = jnp.where(alive, raw, 0.0)
    velocity = particle[...]
    fluid_ref[...] = fluid
    updated_ref[...] = jnp.where(
        alive, velocity + relax[...].reshape(1, slots) * (fluid - velocity), velocity
    )


def sent(values, axis, pairs):
    return lax.ppermute(values, axis, pairs)


def per_device(
    velocity, row_owner, cell_list, weights, offsets, relax_rate, particle_velocity, live_counts
):
    components, x_cells, lines = velocity.shape
    slots = weights.shape[1]
    columns = lax.axis_size("gx")
    owners = lax.axis_size("gy")
    blocks = lines // ROWB
    xor = owners & (owners - 1) == 0
    vmem = pl.BlockSpec(memory_space=pltpu.VMEM)
    smem = pl.BlockSpec(memory_space=pltpu.SMEM)
    hbm = pl.BlockSpec(memory_space=pltpu.HBM)
    limit = 24 * 1024 * 1024
    one = lambda shape: pl.BlockSpec(shape, lambda i: (0,) * len(shape))

    last = x_cells // EDGE - 1
    request, to_chip, to_next = pl.pallas_call(
        lambda *refs: prep_body(x_cells, *refs),
        grid=(1,),
        in_specs=[
            smem,
            pl.BlockSpec((3, EDGE, lines), lambda i: (0, 0, 0)),
            pl.BlockSpec((3, EDGE, lines), lambda i: (0, last, 0)),
            one((STEN, slots)),
            one((STEN, slots)),
            one((slots,)),
        ],
        out_specs=[vmem] * 3,
        out_shape=[
            jax.ShapeDtypeStruct((32, slots), BF16),
            jax.ShapeDtypeStruct((8, lines), F32),
            jax.ShapeDtypeStruct((8, lines), F32),
        ],
        name="prepare",
    )(live_counts, velocity, velocity, cell_list, weights, offsets)

    after = [(i + 1) % columns if i % 2 else (i - 1) % columns for i in range(columns)]
    from_next = sent(to_next, "gx", [(i, after[i]) for i in range(columns)])
    from_chip = sent(to_chip, "gx", [(i, i ^ 1) for i in range(columns)])

    def peer(i, k):
        return i ^ k if xor else (i + k) % owners

    requests = [request] + [
        sent(request, "gy", [(peer(i, k), i) for i in range(owners)]) for k in range(1, owners)
    ]

    window = min(256, x_cells)
    plan, kinds = [], []
    for row in range(0, x_cells, ROWS):
        start = min(max(row - EDGE, 0), x_cells - window)
        if row - start not in kinds:
            kinds.append(row - start)
        plan.append((row, start, kinds.index(row - start)))
    matrices = jnp.asarray(np.stack([toeplitz(o, ROWS, window) for o in kinds]))
    width = 3 * ROWB
    held, table = pl.pallas_call(
        lambda *refs: table_body(plan, *refs),
        in_specs=[hbm, vmem],
        out_specs=[vmem, vmem],
        out_shape=[
            jax.ShapeDtypeStruct(velocity.shape, F32),
            jax.ShapeDtypeStruct((blocks, 2 * width, x_cells), BF16),
        ],
        scratch_shapes=[pltpu.SemaphoreType.DMA((3,))],
        compiler_params=pltpu.CompilerParams(vmem_limit_bytes=LOAD * 1024 * 1024),
        cost_estimate=pl.CostEstimate(
            flops=2 * window * velocity.size, bytes_accessed=8 * velocity.size, transcendentals=0
        ),
        name="table",
    )(velocity, matrices)

    *partials, sides = pl.pallas_call(
        lambda *refs: lookup_body(owners, xor, *refs),
        in_specs=[smem] + [vmem] * (3 + owners),
        out_specs=[vmem] * (owners + 1),
        out_shape=[jax.ShapeDtypeStruct((8, slots), F32)] * owners
        + [jax.ShapeDtypeStruct((16, lines), F32)],
        scratch_shapes=[
            pltpu.VMEM((owners, 32, slots), BF16),
            pltpu.VMEM((blocks, 1, slots), F32),
            pltpu.VMEM((owners, 16, slots), F32),
            pltpu.VMEM((blocks, ROWB, 16), BF16),
            pltpu.SMEM((blocks,), jnp.int32),
        ],
        compiler_params=pltpu.CompilerParams(vmem_limit_bytes=limit),
        cost_estimate=pl.CostEstimate(
            flops=2 * 768 * 6 * x_cells * 1024, bytes_accessed=2 * velocity.size, transcendentals=0
        ),
        name="lookup",
    )(row_owner, from_next, from_chip, table, *requests)

    gradient = pl.pallas_call(
        lambda *refs: derivative_body(plan, *refs),
        in_specs=[vmem] * 3,
        out_specs=hbm,
        out_shape=jax.ShapeDtypeStruct(velocity.shape, F32),
        scratch_shapes=[
            pltpu.VMEM(velocity.shape, F32),
            pltpu.SemaphoreType.DMA((3 * len(plan),)),
        ],
        compiler_params=pltpu.CompilerParams(vmem_limit_bytes=limit),
        cost_estimate=pl.CostEstimate(
            flops=6 * window * velocity.size, bytes_accessed=8 * velocity.size, transcendentals=0
        ),
        name="derivative",
    )(held, matrices, sides)

    returned = [partials[0]] + [
        sent(partials[k], "gy", [(i, peer(i, k)) for i in range(owners)]) for k in range(1, owners)
    ]
    shape = jax.ShapeDtypeStruct((3, slots), F32)
    fluid, updated = pl.pallas_call(
        final_body,
        in_specs=[vmem] * (3 + owners),
        out_specs=[vmem] * 2,
        out_shape=[shape, shape],
        compiler_params=pltpu.CompilerParams(vmem_limit_bytes=limit),
        name="finish",
    )(request, relax_rate, particle_velocity, *returned)
    return (gradient, fluid, updated)


def solution(mesh):
    return jax.shard_map(
        per_device,
        mesh=mesh,
        in_specs=(
            P(None, "gx", "gy"),
            P("gx", None),
            P(None, ("gx", "gy")),
            P(None, ("gx", "gy")),
            P(("gx", "gy")),
            P(("gx", "gy")),
            P(None, ("gx", "gy")),
            P(("gx", "gy")),
        ),
        out_specs=(P(None, "gx", "gy"), P(None, ("gx", "gy")), P(None, ("gx", "gy"))),
        check_vma=False,
    )
```

```python
import math

import jax
import jax.numpy as jnp
import numpy as np
from jax import lax
from jax.experimental import pallas as pl
from jax.experimental.pallas import tpu as pltpu
from jax.sharding import PartitionSpec as P

ROWB = 128
PSIZE = 128
STEN = 4
EDGE = 32
ROWS = 192
CHUNK = 64
EXTRA = 2
LOAD = 43
SCALE = 1.95685
R_DECAY = (3.0 - math.sqrt(5.0)) / 2.0
F32 = jnp.float32
BF16 = jnp.bfloat16


def kernel_taps(reach):
    level = 3.0 / math.sqrt(5.0)

    def inverse(n):
        return level * (-R_DECAY) ** abs(n)

    taps = np.zeros(reach + 1)
    for n in range(reach + 1):
        taps[n] = (7.0 / 9.0) * (inverse(n + 1) - inverse(n - 1)) + (1.0 / 36.0) * (
            inverse(n + 2) - inverse(n - 2)
        )
    return taps


TAPS = kernel_taps(600)
TAIL = TAPS[2] / R_DECAY**2
FIRST = TAPS[1] + TAIL * R_DECAY


def split(values, terms):
    parts = []
    for _ in range(terms):
        part = values.astype(BF16)
        parts.append(part)
        values = values - part.astype(F32)
    return parts


def toeplitz(offset, rows, window):
    distance = offset + np.arange(rows)[:, None] - np.arange(window)[None, :]
    return (np.sign(distance) * TAPS[np.abs(distance)] / SCALE).astype(BF16)


def edge_state(rows, from_first):
    index = lax.broadcasted_iota(jnp.int32, rows.shape, 0)
    steps = index + 1 if from_first else EDGE - index
    parity = 1.0 - 2.0 * (steps & 1).astype(F32)
    decay = parity * jnp.exp(steps.astype(F32) * math.log(R_DECAY))
    return jnp.sum(rows * decay, 0, keepdims=True)


def even_column():
    return lax.rem(lax.axis_index("gx"), 2) == 0


def neighbours(chip_ref, next_ref):
    is_even = even_column()
    chip, following = chip_ref[...], next_ref[...]
    return jnp.where(is_even, following, chip), jnp.where(is_even, chip, following)


def prep_body(x_cells, live, head, tail, cells, weights, offsets, request, to_chip, to_next):
    zero = jnp.zeros((2, head.shape[2]), F32)
    to_left = jnp.concatenate(
        [edge_state(head[c], True) for c in range(3)] + [head[c, 0:1, :] for c in range(3)] + [zero], 0
    )
    to_right = jnp.concatenate(
        [edge_state(tail[c], False) for c in range(3)]
        + [tail[c, EDGE - 1 : EDGE, :] for c in range(3)]
        + [zero],
        0,
    )
    is_even = even_column()
    to_chip[...] = jnp.where(is_even, to_right, to_left)
    to_next[...] = jnp.where(is_even, to_left, to_right)
    cell = cells[...]
    slots = cell.shape[1]
    row = jnp.floor((cell.astype(F32) + 0.5) * (1.0 / x_cells)).astype(jnp.int32)
    x = cell - row * x_cells
    line = row & (ROWB - 1)
    slot = (row >> 7)[0:1]
    lane = lax.broadcasted_iota(jnp.int32, (1, slots), 1)
    limit = jnp.zeros((1, slots), jnp.int32)
    counts = live[...].reshape(1, slots // PSIZE)
    for k in range(slots // PSIZE):
        limit = jnp.where(lane // PSIZE == k, counts[:, k : k + 1], limit)
    alive = lane % PSIZE < limit
    key = jnp.where(alive, slot, -1).astype(F32)
    w_high, w_low = split(weights[...], 2)
    o_high, o_low = split(offsets[...].reshape(1, slots), 2)
    request[...] = jnp.concatenate(
        [
            (x >> 3).astype(F32),
            (x & 7).astype(F32),
            line.astype(F32),
            w_high.astype(F32),
            w_low.astype(F32),
            o_high.astype(F32),
            o_low.astype(F32),
            key,
            jnp.zeros((9, slots), F32),
        ],
        0,
    ).astype(BF16)


def table_body(plan, v_ref, t_ref, held_ref, table_ref, sems):
    window = t_ref.shape[2]
    lines = v_ref.shape[2]
    width = 3 * ROWB
    copies = [pltpu.make_async_copy(v_ref.at[c], held_ref.at[c], sems.at[c]) for c in range(3)]
    for copy in copies:
        copy.start()
    for c in range(3):
        copies[c].wait()
        high = held_ref[c].astype(BF16)
        rows = [
            jnp.dot(t_ref[kind], high[start : start + window], preferred_element_type=F32)
            for row, start, kind in plan
        ]
        slopes = jnp.concatenate([(SCALE * r).astype(BF16) for r in rows], 0)
        for b in range(lines // ROWB):
            at = slice(b * ROWB, (b + 1) * ROWB)
            table_ref[b, c * ROWB : (c + 1) * ROWB] = jnp.transpose(high[:, at])
            table_ref[b, width + c * ROWB : width + (c + 1) * ROWB] = jnp.transpose(slopes[:, at])


def derivative_body(plan, v_ref, t_ref, sides_ref, g_ref, out_buf, sems):
    left, right = sides_ref[:8], sides_ref[8:]
    window = t_ref.shape[2]
    x_cells = v_ref.shape[1]
    copies = []
    for c in range(3):
        high, low = split(v_ref[c], 2)
        sent_to = 0
        for number, (row, start, kind) in enumerate(plan):
            matrix = t_ref[kind]
            both = jnp.concatenate([high[start : start + window], low[start : start + window]], 0)
            out = SCALE * jnp.dot(
                jnp.concatenate([matrix, matrix], 1), both, preferred_element_type=F32
            )
            out_buf[c, row : row + ROWS] = out
            if row == 0:
                out_buf[c, :EDGE] = edge_fix(out[:EDGE], left[c : c + 1], left[c + 3 : c + 4], True)
            if row + ROWS == x_cells:
                out_buf[c, x_cells - EDGE :] = edge_fix(
                    out_buf[c, x_cells - EDGE :], right[c : c + 1], right[c + 3 : c + 4], False
                )
            if number % 2 == 1 or row + ROWS == x_cells:
                rows = pl.ds(sent_to, row + ROWS - sent_to)
                sent_to = row + ROWS
                copy = pltpu.make_async_copy(
                    out_buf.at[c, rows], g_ref.at[c, rows], sems.at[len(copies)]
                )
                copy.start()
                copies.append(copy)
    for copy in copies:
        copy.wait()


def edge_fix(rows, state, plane, is_left):
    index = lax.broadcasted_iota(jnp.int32, rows.shape, 0)
    steps = index if is_left else EDGE - 1 - index
    parity = 1.0 - 2.0 * (steps & 1).astype(F32)
    decay = parity * jnp.exp(steps.astype(F32) * math.log(R_DECAY))
    sign = 1.0 if is_left else -1.0
    return rows + (sign * TAIL) * decay * state + jnp.where(steps == 0, sign * FIRST, 0.0) * plane


def signed_decay(steps):
    parity = 1.0 - 2.0 * (steps.astype(jnp.int32) & 1).astype(F32)
    return parity * jnp.exp(steps * math.log(R_DECAY))


def lookup_body(owners, xor, owner_ref, next_ref, chip_ref, table_ref, *refs):
    request_refs = refs[:owners]
    out_refs = refs[owners : 2 * owners]
    sides_ref = refs[2 * owners]
    requests, ranks, totals, states, peer_at = refs[2 * owners + 1 :]
    blocks, _, x_cells = table_ref.shape
    width = 3 * ROWB
    me = lax.axis_index("gy")
    capacity = blocks // 2
    slots = requests.shape[2]
    groups = slots // ROWB
    cells = STEN * CHUNK

    row_owners = owner_ref[...].astype(F32)
    row_lane = lax.broadcasted_iota(jnp.int32, row_owners.shape, 1)
    peers = []
    for block in range(blocks):
        mine = jnp.where(row_lane == me * blocks + block, row_owners, 0.0)
        owner = jnp.sum(mine).astype(jnp.int32)
        peers.append((owner ^ me) if xor else lax.rem(owner - me + owners, owners))
        peer_at[block] = peers[block]
    for k in range(owners):
        requests[k] = request_refs[k][...]
        totals[k] = jnp.zeros(totals.shape[1:], F32)
    sides = jnp.concatenate(neighbours(chip_ref, next_ref), 0)
    sides_ref[...] = sides
    for block in range(blocks):
        states[block] = jnp.transpose(sides[:, block * ROWB : (block + 1) * ROWB]).astype(BF16)

    matched = []
    for block in range(blocks):
        rank = jnp.int32(0)
        for earlier in range(block):
            rank += (peers[earlier] == peers[block]).astype(jnp.int32)
        key = requests[peers[block], 16:32, :].astype(F32)[6:7]
        matched.append(jnp.where(key == (me * capacity + rank).astype(F32), 1.0, 0.0))
    stacked = jnp.concatenate(
        [m[:, k * ROWB : (k + 1) * ROWB] for m in matched for k in range(groups)], 0
    )
    upto = lax.broadcasted_iota(jnp.int32, (ROWB, ROWB), 0) <= lax.broadcasted_iota(
        jnp.int32, (ROWB, ROWB), 1
    )
    running = jnp.dot(
        stacked.astype(BF16), jnp.where(upto, 1.0, 0.0).astype(BF16), preferred_element_type=F32
    )
    ends = []
    end = jnp.int32(0)
    for block in range(blocks):
        before = jnp.zeros((1, 1), F32)
        pieces = []
        for k in range(groups):
            r = block * groups + k
            line = running[r : r + 1]
            pieces.append(jnp.where(stacked[r : r + 1] > 0.5, line - 1.0 + before, -1.0))
            before = before + line[:, ROWB - 1 : ROWB]
        ranks[block] = jnp.concatenate(pieces, 1)
        count = before[0, 0].astype(jnp.int32)
        end = end + jnp.maximum((count + CHUNK - 1) // CHUNK - 1, 0)
        ends.append(end)

    x_iota = lax.broadcasted_iota(jnp.int32, (x_cells, cells), 0).astype(F32)
    line_iota = lax.broadcasted_iota(jnp.int32, (ROWB, cells), 0).astype(F32)
    state_iota = lax.broadcasted_iota(jnp.int32, (16, cells), 0)
    place = lax.broadcasted_iota(jnp.int32, (CHUNK, slots), 0)
    low_half = lax.broadcasted_iota(jnp.int32, (1, 2 * CHUNK), 1) < CHUNK

    def batch(tasks):
        chosen, data = [], []
        for block, peer, i in tasks:
            one = jnp.where(ranks[block] == (place + i * CHUNK).astype(F32), 1.0, 0.0).astype(BF16)
            chosen.append(jnp.concatenate([one, one], 0))
        for (block, peer, i), pick in zip(tasks, chosen):
            data.append(
                lax.dot_general(
                    requests[peer], pick, (((1,), (1,)), ((), ())), preferred_element_type=F32
                )
            )
        found, halos, masks, offsets = [], [], [], []
        for (block, peer, i), d in zip(tasks, data):

            def by_cell(row):
                pairs = [
                    jnp.where(low_half, d[row + s : row + s + 1], d[row + s + 1 : row + s + 2])
                    for s in (0, 2)
                ]
                return jnp.concatenate(pairs, 1)

            x = by_cell(0) * 8.0 + by_cell(4)
            weight = by_cell(12) + by_cell(16)
            offset = d[20:21] + d[21:22]
            offsets.append(jnp.concatenate([offset, offset], 1))
            masks.append(jnp.where(line_iota == by_cell(8), weight, 0.0))
            pick = jnp.where(x_iota == x, 1.0, 0.0).astype(BF16)
            found.append(jnp.dot(table_ref[block], pick, preferred_element_type=F32))
            y = x_cells - 1.0 - x
            left = jnp.where(x < EDGE, TAIL * signed_decay(x), 0.0)
            right = jnp.where(y < EDGE, -TAIL * signed_decay(y), 0.0)
            left_first = jnp.where(x == 0.0, FIRST, 0.0)
            right_first = jnp.where(y == 0.0, -FIRST, 0.0)
            terms = []
            for c in range(3):
                term = jnp.where(state_iota == c, left, 0.0)
                term = jnp.where(state_iota == c + 3, left_first, term)
                term = jnp.where(state_iota == c + 8, right, term)
                terms.append(jnp.where(state_iota == c + 11, right_first, term))
            halos.append(
                jnp.dot(
                    states[block],
                    jnp.concatenate(terms, 1).astype(BF16),
                    preferred_element_type=F32,
                )
            )
        for (block, peer, i), f, h, mask, offset, pick in zip(
            tasks, found, halos, masks, offsets, chosen
        ):
            sums = []
            for c in range(3):
                carried = f[c * ROWB : (c + 1) * ROWB]
                slope = f[width + c * ROWB : width + (c + 1) * ROWB]
                slope = slope + h[:, c * cells : (c + 1) * cells]
                sums.append(jnp.sum((carried + offset * slope) * mask, 0, keepdims=True))
            sums.append(jnp.zeros((1, cells), F32))
            value = jnp.concatenate(sums, 0)
            value = value[:, : 2 * CHUNK] + value[:, 2 * CHUNK :]
            back = jnp.concatenate(
                [p.astype(F32) for p in split(value, 3)] + [jnp.zeros((4, 2 * CHUNK), F32)], 0
            )
            totals[peer] += jnp.dot(back.astype(BF16), pick, preferred_element_type=F32)

    def extra(number):
        block = jnp.int32(0)
        first = jnp.int32(0)
        for b in range(blocks - 1):
            past = number >= ends[b]
            block = jnp.where(past, b + 1, block)
            first = jnp.where(past, ends[b], first)
        return block, peer_at[block], number - first + 1

    base = [(block, peers[block], jnp.int32(0)) for block in range(blocks)]
    extras = ends[-1]
    sizes = [0, EXTRA, 2 * EXTRA]
    for size, above in zip(sizes, sizes[1:] + [None]):
        fits = extras > size - EXTRA
        if above is not None:
            fits = jnp.logical_and(fits, extras <= size)

        @pl.when(fits)
        def _(size=size):
            batch(base + [extra(jnp.int32(t)) for t in range(size)])

    @pl.loop(2, (extras + EXTRA - 1) // EXTRA)
    def _(i):
        batch([extra(i * EXTRA + t) for t in range(EXTRA)])

    for k in range(owners):
        total = totals[k]
        out_refs[k][...] = total[0:8] + pltpu.roll(total[0:8], 4, 0) + total[8:16]


def final_body(request, relax, particle, *refs):
    parts, (fluid_ref, updated_ref) = refs[:-2], refs[-2:]
    raw = parts[0][0:3]
    for part in parts[1:]:
        raw = raw + part[0:3]
    slots = raw.shape[1]
    alive = jnp.broadcast_to(request[16:32].astype(F32)[6:7], raw.shape) >= 0.0
    fluid = jnp.where(alive, raw, 0.0)
    velocity = particle[...]
    fluid_ref[...] = fluid
    updated_ref[...] = jnp.where(
        alive, velocity + relax[...].reshape(1, slots) * (fluid - velocity), velocity
    )


def sent(values, axis, pairs):
    return lax.ppermute(values, axis, pairs)


def per_device(
    velocity, row_owner, cell_list, weights, offsets, relax_rate, particle_velocity, live_counts
):
    components, x_cells, lines = velocity.shape
    slots = weights.shape[1]
    columns = lax.axis_size("gx")
    owners = lax.axis_size("gy")
    blocks = lines // ROWB
    xor = owners & (owners - 1) == 0
    vmem = pl.BlockSpec(memory_space=pltpu.VMEM)
    smem = pl.BlockSpec(memory_space=pltpu.SMEM)
    hbm = pl.BlockSpec(memory_space=pltpu.HBM)
    limit = 24 * 1024 * 1024
    one = lambda shape: pl.BlockSpec(shape, lambda i: (0,) * len(shape))

    last = x_cells // EDGE - 1
    request, to_chip, to_next = pl.pallas_call(
        lambda *refs: prep_body(x_cells, *refs),
        grid=(1,),
        in_specs=[
            one((slots // PSIZE,)),
            pl.BlockSpec((3, EDGE, lines), lambda i: (0, 0, 0)),
            pl.BlockSpec((3, EDGE, lines), lambda i: (0, last, 0)),
            one((STEN, slots)),
            one((STEN, slots)),
            one((slots,)),
        ],
        out_specs=[vmem] * 3,
        out_shape=[
            jax.ShapeDtypeStruct((32, slots), BF16),
            jax.ShapeDtypeStruct((8, lines), F32),
            jax.ShapeDtypeStruct((8, lines), F32),
        ],
        name="prepare",
    )(live_counts, velocity, velocity, cell_list, weights, offsets)

    after = [(i + 1) % columns if i % 2 else (i - 1) % columns for i in range(columns)]
    from_next = sent(to_next, "gx", [(i, after[i]) for i in range(columns)])
    from_chip = sent(to_chip, "gx", [(i, i ^ 1) for i in range(columns)])

    def peer(i, k):
        return i ^ k if xor else (i + k) % owners

    requests = [request] + [
        sent(request, "gy", [(peer(i, k), i) for i in range(owners)]) for k in range(1, owners)
    ]

    window = min(256, x_cells)
    plan, kinds = [], []
    for row in range(0, x_cells, ROWS):
        start = min(max(row - EDGE, 0), x_cells - window)
        if row - start not in kinds:
            kinds.append(row - start)
        plan.append((row, start, kinds.index(row - start)))
    matrices = jnp.asarray(np.stack([toeplitz(o, ROWS, window) for o in kinds]))
    width = 3 * ROWB
    held, table = pl.pallas_call(
        lambda *refs: table_body(plan, *refs),
        in_specs=[hbm, vmem],
        out_specs=[vmem, vmem],
        out_shape=[
            jax.ShapeDtypeStruct(velocity.shape, F32),
            jax.ShapeDtypeStruct((blocks, 2 * width, x_cells), BF16),
        ],
        scratch_shapes=[pltpu.SemaphoreType.DMA((3,))],
        compiler_params=pltpu.CompilerParams(vmem_limit_bytes=LOAD * 1024 * 1024),
        cost_estimate=pl.CostEstimate(
            flops=2 * window * velocity.size, bytes_accessed=8 * velocity.size, transcendentals=0
        ),
        name="table",
    )(velocity, matrices)

    *partials, sides = pl.pallas_call(
        lambda *refs: lookup_body(owners, xor, *refs),
        in_specs=[vmem] * (4 + owners),
        out_specs=[vmem] * (owners + 1),
        out_shape=[jax.ShapeDtypeStruct((8, slots), F32)] * owners
        + [jax.ShapeDtypeStruct((16, lines), F32)],
        scratch_shapes=[
            pltpu.VMEM((owners, 32, slots), BF16),
            pltpu.VMEM((blocks, 1, slots), F32),
            pltpu.VMEM((owners, 16, slots), F32),
            pltpu.VMEM((blocks, ROWB, 16), BF16),
            pltpu.SMEM((blocks,), jnp.int32),
        ],
        compiler_params=pltpu.CompilerParams(vmem_limit_bytes=limit),
        cost_estimate=pl.CostEstimate(
            flops=2 * 768 * 6 * x_cells * 1024, bytes_accessed=2 * velocity.size, transcendentals=0
        ),
        name="lookup",
    )(row_owner, from_next, from_chip, table, *requests)

    gradient = pl.pallas_call(
        lambda *refs: derivative_body(plan, *refs),
        in_specs=[vmem] * 3,
        out_specs=hbm,
        out_shape=jax.ShapeDtypeStruct(velocity.shape, F32),
        scratch_shapes=[
            pltpu.VMEM(velocity.shape, F32),
            pltpu.SemaphoreType.DMA((3 * len(plan),)),
        ],
        compiler_params=pltpu.CompilerParams(vmem_limit_bytes=limit),
        cost_estimate=pl.CostEstimate(
            flops=6 * window * velocity.size, bytes_accessed=8 * velocity.size, transcendentals=0
        ),
        name="derivative",
    )(held, matrices, sides)

    returned = [partials[0]] + [
        sent(partials[k], "gy", [(i, peer(i, k)) for i in range(owners)]) for k in range(1, owners)
    ]
    shape = jax.ShapeDtypeStruct((3, slots), F32)
    fluid, updated = pl.pallas_call(
        final_body,
        in_specs=[vmem] * (3 + owners),
        out_specs=[vmem] * 2,
        out_shape=[shape, shape],
        compiler_params=pltpu.CompilerParams(vmem_limit_bytes=limit),
        name="finish",
    )(request, relax_rate, particle_velocity, *returned)
    return (gradient, fluid, updated)


def solution(mesh):
    return jax.shard_map(
        per_device,
        mesh=mesh,
        in_specs=(
            P(None, "gx", "gy"),
            P("gx", None),
            P(None, ("gx", "gy")),
            P(None, ("gx", "gy")),
            P(("gx", "gy")),
            P(("gx", "gy")),
            P(None, ("gx", "gy")),
            P(("gx", "gy")),
        ),
        out_specs=(P(None, "gx", "gy"), P(None, ("gx", "gy")), P(None, ("gx", "gy"))),
        check_vma=False,
    )
```

```python
import math

import jax
import jax.numpy as jnp
import numpy as np
from jax import lax
from jax.experimental import pallas as pl
from jax.experimental.pallas import tpu as pltpu
from jax.sharding import PartitionSpec as P

ROWB = 128
PSIZE = 128
STEN = 4
EDGE = 32
ROWS = 192
CHUNK = 64
EXTRA = 2
LOAD = 43
SCALE = 1.95685
R_DECAY = (3.0 - math.sqrt(5.0)) / 2.0
F32 = jnp.float32
BF16 = jnp.bfloat16


def kernel_taps(reach):
    level = 3.0 / math.sqrt(5.0)

    def inverse(n):
        return level * (-R_DECAY) ** abs(n)

    taps = np.zeros(reach + 1)
    for n in range(reach + 1):
        taps[n] = (7.0 / 9.0) * (inverse(n + 1) - inverse(n - 1)) + (1.0 / 36.0) * (
            inverse(n + 2) - inverse(n - 2)
        )
    return taps


TAPS = kernel_taps(600)
TAIL = TAPS[2] / R_DECAY**2
FIRST = TAPS[1] + TAIL * R_DECAY


def split(values, terms):
    parts = []
    for _ in range(terms):
        part = values.astype(BF16)
        parts.append(part)
        values = values - part.astype(F32)
    return parts


def toeplitz(offset, rows, window):
    distance = offset + np.arange(rows)[:, None] - np.arange(window)[None, :]
    return (np.sign(distance) * TAPS[np.abs(distance)] / SCALE).astype(BF16)


def edge_state(rows, from_first):
    index = lax.broadcasted_iota(jnp.int32, rows.shape, 0)
    steps = index + 1 if from_first else EDGE - index
    parity = 1.0 - 2.0 * (steps & 1).astype(F32)
    decay = parity * jnp.exp(steps.astype(F32) * math.log(R_DECAY))
    return jnp.sum(rows * decay, 0, keepdims=True)


def even_column():
    return lax.rem(lax.axis_index("gx"), 2) == 0


def neighbours(chip_ref, next_ref):
    is_even = even_column()
    chip, following = chip_ref[...], next_ref[...]
    return jnp.where(is_even, following, chip), jnp.where(is_even, chip, following)


def prep_body(x_cells, live, head, tail, cells, weights, offsets, request, to_chip, to_next):
    zero = jnp.zeros((2, head.shape[2]), F32)
    to_left = jnp.concatenate(
        [edge_state(head[c], True) for c in range(3)] + [head[c, 0:1, :] for c in range(3)] + [zero], 0
    )
    to_right = jnp.concatenate(
        [edge_state(tail[c], False) for c in range(3)]
        + [tail[c, EDGE - 1 : EDGE, :] for c in range(3)]
        + [zero],
        0,
    )
    is_even = even_column()
    to_chip[...] = jnp.where(is_even, to_right, to_left)
    to_next[...] = jnp.where(is_even, to_left, to_right)
    cell = cells[...]
    slots = cell.shape[1]
    row = jnp.floor((cell.astype(F32) + 0.5) * (1.0 / x_cells)).astype(jnp.int32)
    x = cell - row * x_cells
    line = row & (ROWB - 1)
    slot = (row >> 7)[0:1]
    lane = lax.broadcasted_iota(jnp.int32, (1, slots), 1)
    limit = jnp.zeros((1, slots), jnp.int32)
    counts = live[...].reshape(1, slots // PSIZE)
    for k in range(slots // PSIZE):
        limit = jnp.where(lane // PSIZE == k, counts[:, k : k + 1], limit)
    alive = lane % PSIZE < limit
    key = jnp.where(alive, slot, -1).astype(F32)
    w_high, w_low = split(weights[...], 2)
    o_high, o_low = split(offsets[...].reshape(1, slots), 2)
    request[...] = jnp.concatenate(
        [
            (x >> 3).astype(F32),
            (x & 7).astype(F32),
            line.astype(F32),
            w_high.astype(F32),
            w_low.astype(F32),
            o_high.astype(F32),
            o_low.astype(F32),
            key,
            jnp.zeros((9, slots), F32),
        ],
        0,
    ).astype(BF16)


def table_body(plan, v_ref, t_ref, held_ref, table_ref, sems):
    window = t_ref.shape[2]
    lines = v_ref.shape[2]
    width = 3 * ROWB
    copies = [pltpu.make_async_copy(v_ref.at[c], held_ref.at[c], sems.at[c]) for c in range(3)]
    for copy in copies:
        copy.start()
    for c in range(3):
        copies[c].wait()
        high = held_ref[c].astype(BF16)
        rows = [
            jnp.dot(t_ref[kind], high[start : start + window], preferred_element_type=F32)
            for row, start, kind in plan
        ]
        slopes = jnp.concatenate([(SCALE * r).astype(BF16) for r in rows], 0)
        for b in range(lines // ROWB):
            at = slice(b * ROWB, (b + 1) * ROWB)
            table_ref[b, c * ROWB : (c + 1) * ROWB] = jnp.transpose(high[:, at])
            table_ref[b, width + c * ROWB : width + (c + 1) * ROWB] = jnp.transpose(slopes[:, at])


def derivative_body(plan, v_ref, t_ref, sides_ref, g_ref, out_buf, sems):
    left, right = sides_ref[:8], sides_ref[8:]
    window = t_ref.shape[2]
    x_cells = v_ref.shape[1]
    copies = []
    for c in range(3):
        high, low = split(v_ref[c], 2)
        sent_to = 0
        for number, (row, start, kind) in enumerate(plan):
            matrix = t_ref[kind]
            both = jnp.concatenate([high[start : start + window], low[start : start + window]], 0)
            out = SCALE * jnp.dot(
                jnp.concatenate([matrix, matrix], 1), both, preferred_element_type=F32
            )
            out_buf[c, row : row + ROWS] = out
            if row == 0:
                out_buf[c, :EDGE] = edge_fix(out[:EDGE], left[c : c + 1], left[c + 3 : c + 4], True)
            if row + ROWS == x_cells:
                out_buf[c, x_cells - EDGE :] = edge_fix(
                    out_buf[c, x_cells - EDGE :], right[c : c + 1], right[c + 3 : c + 4], False
                )
            if number % 2 == 1 or row + ROWS == x_cells:
                rows = pl.ds(sent_to, row + ROWS - sent_to)
                sent_to = row + ROWS
                copy = pltpu.make_async_copy(
                    out_buf.at[c, rows], g_ref.at[c, rows], sems.at[len(copies)]
                )
                copy.start()
                copies.append(copy)
    for copy in copies:
        copy.wait()


def edge_fix(rows, state, plane, is_left):
    index = lax.broadcasted_iota(jnp.int32, rows.shape, 0)
    steps = index if is_left else EDGE - 1 - index
    parity = 1.0 - 2.0 * (steps & 1).astype(F32)
    decay = parity * jnp.exp(steps.astype(F32) * math.log(R_DECAY))
    sign = 1.0 if is_left else -1.0
    return rows + (sign * TAIL) * decay * state + jnp.where(steps == 0, sign * FIRST, 0.0) * plane


def signed_decay(steps):
    parity = 1.0 - 2.0 * (steps.astype(jnp.int32) & 1).astype(F32)
    return parity * jnp.exp(steps * math.log(R_DECAY))


def lookup_body(owners, xor, order, owner_ref, next_ref, chip_ref, table_ref, *refs):
    request_refs = refs[:owners]
    out_refs = refs[owners : 2 * owners]
    sides_ref = refs[2 * owners]
    requests, ranks, totals, states, peer_at = refs[2 * owners + 1 :]
    blocks, _, x_cells = table_ref.shape
    width = 3 * ROWB
    me = lax.axis_index("gy")
    capacity = blocks // 2
    slots = requests.shape[2]
    groups = slots // ROWB
    cells = STEN * CHUNK

    row_owners = owner_ref[...].astype(F32)
    row_lane = lax.broadcasted_iota(jnp.int32, row_owners.shape, 1)
    peers = []
    for block in range(blocks):
        mine = jnp.where(row_lane == me * blocks + block, row_owners, 0.0)
        owner = jnp.sum(mine).astype(jnp.int32)
        peers.append((owner ^ me) if xor else lax.rem(owner - me + owners, owners))
        peer_at[block] = peers[block]
    for k in range(owners):
        requests[order[k]] = request_refs[k][...]
        totals[k] = jnp.zeros(totals.shape[1:], F32)
    sides = jnp.concatenate(neighbours(chip_ref, next_ref), 0)
    sides_ref[...] = sides
    for block in range(blocks):
        states[block] = jnp.transpose(sides[:, block * ROWB : (block + 1) * ROWB]).astype(BF16)

    matched = []
    for block in range(blocks):
        rank = jnp.int32(0)
        for earlier in range(block):
            rank += (peers[earlier] == peers[block]).astype(jnp.int32)
        key = requests[peers[block], 16:32, :].astype(F32)[6:7]
        matched.append(jnp.where(key == (me * capacity + rank).astype(F32), 1.0, 0.0))
    stacked = jnp.concatenate(
        [m[:, k * ROWB : (k + 1) * ROWB] for m in matched for k in range(groups)], 0
    )
    upto = lax.broadcasted_iota(jnp.int32, (ROWB, ROWB), 0) <= lax.broadcasted_iota(
        jnp.int32, (ROWB, ROWB), 1
    )
    running = jnp.dot(
        stacked.astype(BF16), jnp.where(upto, 1.0, 0.0).astype(BF16), preferred_element_type=F32
    )
    ends = []
    end = jnp.int32(0)
    for block in range(blocks):
        before = jnp.zeros((1, 1), F32)
        pieces = []
        for k in range(groups):
            r = block * groups + k
            line = running[r : r + 1]
            pieces.append(jnp.where(stacked[r : r + 1] > 0.5, line - 1.0 + before, -1.0))
            before = before + line[:, ROWB - 1 : ROWB]
        ranks[block] = jnp.concatenate(pieces, 1)
        count = before[0, 0].astype(jnp.int32)
        end = end + jnp.maximum((count + CHUNK - 1) // CHUNK - 1, 0)
        ends.append(end)

    x_iota = lax.broadcasted_iota(jnp.int32, (x_cells, cells), 0).astype(F32)
    line_iota = lax.broadcasted_iota(jnp.int32, (ROWB, cells), 0).astype(F32)
    state_iota = lax.broadcasted_iota(jnp.int32, (16, cells), 0)
    place = lax.broadcasted_iota(jnp.int32, (CHUNK, slots), 0)
    low_half = lax.broadcasted_iota(jnp.int32, (1, 2 * CHUNK), 1) < CHUNK

    def batch(tasks):
        chosen, data = [], []
        for block, peer, i in tasks:
            one = jnp.where(ranks[block] == (place + i * CHUNK).astype(F32), 1.0, 0.0).astype(BF16)
            chosen.append(jnp.concatenate([one, one], 0))
        for (block, peer, i), pick in zip(tasks, chosen):
            data.append(
                lax.dot_general(
                    requests[peer], pick, (((1,), (1,)), ((), ())), preferred_element_type=F32
                )
            )
        found, halos, masks, offsets = [], [], [], []
        for (block, peer, i), d in zip(tasks, data):

            def by_cell(row):
                pairs = [
                    jnp.where(low_half, d[row + s : row + s + 1], d[row + s + 1 : row + s + 2])
                    for s in (0, 2)
                ]
                return jnp.concatenate(pairs, 1)

            x = by_cell(0) * 8.0 + by_cell(4)
            weight = by_cell(12) + by_cell(16)
            offset = d[20:21] + d[21:22]
            offsets.append(jnp.concatenate([offset, offset], 1))
            masks.append(jnp.where(line_iota == by_cell(8), weight, 0.0))
            pick = jnp.where(x_iota == x, 1.0, 0.0).astype(BF16)
            found.append(jnp.dot(table_ref[block], pick, preferred_element_type=F32))
            y = x_cells - 1.0 - x
            left = jnp.where(x < EDGE, TAIL * signed_decay(x), 0.0)
            right = jnp.where(y < EDGE, -TAIL * signed_decay(y), 0.0)
            left_first = jnp.where(x == 0.0, FIRST, 0.0)
            right_first = jnp.where(y == 0.0, -FIRST, 0.0)
            terms = []
            for c in range(3):
                term = jnp.where(state_iota == c, left, 0.0)
                term = jnp.where(state_iota == c + 3, left_first, term)
                term = jnp.where(state_iota == c + 8, right, term)
                terms.append(jnp.where(state_iota == c + 11, right_first, term))
            halos.append(
                jnp.dot(
                    states[block],
                    jnp.concatenate(terms, 1).astype(BF16),
                    preferred_element_type=F32,
                )
            )
        for (block, peer, i), f, h, mask, offset, pick in zip(
            tasks, found, halos, masks, offsets, chosen
        ):
            sums = []
            for c in range(3):
                carried = f[c * ROWB : (c + 1) * ROWB]
                slope = f[width + c * ROWB : width + (c + 1) * ROWB]
                slope = slope + h[:, c * cells : (c + 1) * cells]
                sums.append(jnp.sum((carried + offset * slope) * mask, 0, keepdims=True))
            sums.append(jnp.zeros((1, cells), F32))
            value = jnp.concatenate(sums, 0)
            value = value[:, : 2 * CHUNK] + value[:, 2 * CHUNK :]
            back = jnp.concatenate(
                [p.astype(F32) for p in split(value, 3)] + [jnp.zeros((4, 2 * CHUNK), F32)], 0
            )
            totals[peer] += jnp.dot(back.astype(BF16), pick, preferred_element_type=F32)

    def extra(number):
        block = jnp.int32(0)
        first = jnp.int32(0)
        for b in range(blocks - 1):
            past = number >= ends[b]
            block = jnp.where(past, b + 1, block)
            first = jnp.where(past, ends[b], first)
        return block, peer_at[block], number - first + 1

    base = [(block, peers[block], jnp.int32(0)) for block in range(blocks)]
    extras = ends[-1]
    sizes = [0, EXTRA, 2 * EXTRA]
    for size, above in zip(sizes, sizes[1:] + [None]):
        fits = extras > size - EXTRA
        if above is not None:
            fits = jnp.logical_and(fits, extras <= size)

        @pl.when(fits)
        def _(size=size):
            batch(base + [extra(jnp.int32(t)) for t in range(size)])

    @pl.loop(2, (extras + EXTRA - 1) // EXTRA)
    def _(i):
        batch([extra(i * EXTRA + t) for t in range(EXTRA)])

    for k in range(owners):
        total = totals[k]
        out_refs[k][...] = total[0:8] + pltpu.roll(total[0:8], 4, 0) + total[8:16]


def final_body(request, relax, particle, *refs):
    parts, (fluid_ref, updated_ref) = refs[:-2], refs[-2:]
    raw = parts[0][0:3]
    for part in parts[1:]:
        raw = raw + part[0:3]
    slots = raw.shape[1]
    alive = jnp.broadcast_to(request[16:32].astype(F32)[6:7], raw.shape) >= 0.0
    fluid = jnp.where(alive, raw, 0.0)
    velocity = particle[...]
    fluid_ref[...] = fluid
    updated_ref[...] = jnp.where(
        alive, velocity + relax[...].reshape(1, slots) * (fluid - velocity), velocity
    )


def sent(values, axis, pairs):
    return lax.ppermute(values, axis, pairs)


def per_device(
    velocity, row_owner, cell_list, weights, offsets, relax_rate, particle_velocity, live_counts
):
    components, x_cells, lines = velocity.shape
    slots = weights.shape[1]
    columns = lax.axis_size("gx")
    owners = lax.axis_size("gy")
    blocks = lines // ROWB
    xor = owners & (owners - 1) == 0
    vmem = pl.BlockSpec(memory_space=pltpu.VMEM)
    smem = pl.BlockSpec(memory_space=pltpu.SMEM)
    hbm = pl.BlockSpec(memory_space=pltpu.HBM)
    limit = 24 * 1024 * 1024
    one = lambda shape: pl.BlockSpec(shape, lambda i: (0,) * len(shape))

    last = x_cells // EDGE - 1
    request, to_chip, to_next = pl.pallas_call(
        lambda *refs: prep_body(x_cells, *refs),
        grid=(1,),
        in_specs=[
            one((slots // PSIZE,)),
            pl.BlockSpec((3, EDGE, lines), lambda i: (0, 0, 0)),
            pl.BlockSpec((3, EDGE, lines), lambda i: (0, last, 0)),
            one((STEN, slots)),
            one((STEN, slots)),
            one((slots,)),
        ],
        out_specs=[vmem] * 3,
        out_shape=[
            jax.ShapeDtypeStruct((32, slots), BF16),
            jax.ShapeDtypeStruct((8, lines), F32),
            jax.ShapeDtypeStruct((8, lines), F32),
        ],
        name="prepare",
    )(live_counts, velocity, velocity, cell_list, weights, offsets)

    after = [(i + 1) % columns if i % 2 else (i - 1) % columns for i in range(columns)]
    from_next = sent(to_next, "gx", [(i, after[i]) for i in range(columns)])
    from_chip = sent(to_chip, "gx", [(i, i ^ 1) for i in range(columns)])

    def peer(i, k):
        return i ^ k if xor else (i + k) % owners

    far_first = sorted(range(1, owners), key=lambda k: -bin(k).count("1"))
    requests = [request] + [
        sent(request, "gy", [(peer(i, k), i) for i in range(owners)]) for k in far_first
    ]

    window = min(256, x_cells)
    plan, kinds = [], []
    for row in range(0, x_cells, ROWS):
        start = min(max(row - EDGE, 0), x_cells - window)
        if row - start not in kinds:
            kinds.append(row - start)
        plan.append((row, start, kinds.index(row - start)))
    matrices = jnp.asarray(np.stack([toeplitz(o, ROWS, window) for o in kinds]))
    width = 3 * ROWB
    held, table = pl.pallas_call(
        lambda *refs: table_body(plan, *refs),
        in_specs=[hbm, vmem],
        out_specs=[vmem, vmem],
        out_shape=[
            jax.ShapeDtypeStruct(velocity.shape, F32),
            jax.ShapeDtypeStruct((blocks, 2 * width, x_cells), BF16),
        ],
        scratch_shapes=[pltpu.SemaphoreType.DMA((3,))],
        compiler_params=pltpu.CompilerParams(vmem_limit_bytes=LOAD * 1024 * 1024),
        cost_estimate=pl.CostEstimate(
            flops=2 * window * velocity.size, bytes_accessed=8 * velocity.size, transcendentals=0
        ),
        name="table",
    )(velocity, matrices)

    *partials, sides = pl.pallas_call(
        lambda *refs: lookup_body(owners, xor, [0] + far_first, *refs),
        in_specs=[vmem] * (4 + owners),
        out_specs=[vmem] * (owners + 1),
        out_shape=[jax.ShapeDtypeStruct((8, slots), F32)] * owners
        + [jax.ShapeDtypeStruct((16, lines), F32)],
        scratch_shapes=[
            pltpu.VMEM((owners, 32, slots), BF16),
            pltpu.VMEM((blocks, 1, slots), F32),
            pltpu.VMEM((owners, 16, slots), F32),
            pltpu.VMEM((blocks, ROWB, 16), BF16),
            pltpu.SMEM((blocks,), jnp.int32),
        ],
        compiler_params=pltpu.CompilerParams(vmem_limit_bytes=limit),
        cost_estimate=pl.CostEstimate(
            flops=2 * 768 * 6 * x_cells * 1024, bytes_accessed=2 * velocity.size, transcendentals=0
        ),
        name="lookup",
    )(row_owner, from_next, from_chip, table, *requests)

    gradient = pl.pallas_call(
        lambda *refs: derivative_body(plan, *refs),
        in_specs=[vmem] * 3,
        out_specs=hbm,
        out_shape=jax.ShapeDtypeStruct(velocity.shape, F32),
        scratch_shapes=[
            pltpu.VMEM(velocity.shape, F32),
            pltpu.SemaphoreType.DMA((3 * len(plan),)),
        ],
        compiler_params=pltpu.CompilerParams(vmem_limit_bytes=limit),
        cost_estimate=pl.CostEstimate(
            flops=6 * window * velocity.size, bytes_accessed=8 * velocity.size, transcendentals=0
        ),
        name="derivative",
    )(held, matrices, sides)

    returned = [partials[0]] + [
        sent(partials[k], "gy", [(i, peer(i, k)) for i in range(owners)]) for k in far_first
    ]
    shape = jax.ShapeDtypeStruct((3, slots), F32)
    fluid, updated = pl.pallas_call(
        final_body,
        in_specs=[vmem] * (3 + owners),
        out_specs=[vmem] * 2,
        out_shape=[shape, shape],
        compiler_params=pltpu.CompilerParams(vmem_limit_bytes=limit),
        name="finish",
    )(request, relax_rate, particle_velocity, *returned)
    return (gradient, fluid, updated)


def solution(mesh):
    return jax.shard_map(
        per_device,
        mesh=mesh,
        in_specs=(
            P(None, "gx", "gy"),
            P("gx", None),
            P(None, ("gx", "gy")),
            P(None, ("gx", "gy")),
            P(("gx", "gy")),
            P(("gx", "gy")),
            P(None, ("gx", "gy")),
            P(("gx", "gy")),
        ),
        out_specs=(P(None, "gx", "gy"), P(None, ("gx", "gy")), P(None, ("gx", "gy"))),
        check_vma=False,
    )
```

```python
import math

import jax
import jax.numpy as jnp
import numpy as np
from jax import lax
from jax.experimental import pallas as pl
from jax.experimental.pallas import tpu as pltpu
from jax.sharding import PartitionSpec as P

ROWB = 128
PSIZE = 128
STEN = 4
EDGE = 24
ROWS = 192
CHUNK = 64
EXTRA = 2
LOAD = 43
SCALE = 1.95685
R_DECAY = (3.0 - math.sqrt(5.0)) / 2.0
F32 = jnp.float32
BF16 = jnp.bfloat16


def kernel_taps(reach):
    level = 3.0 / math.sqrt(5.0)

    def inverse(n):
        return level * (-R_DECAY) ** abs(n)

    taps = np.zeros(reach + 1)
    for n in range(reach + 1):
        taps[n] = (7.0 / 9.0) * (inverse(n + 1) - inverse(n - 1)) + (1.0 / 36.0) * (
            inverse(n + 2) - inverse(n - 2)
        )
    return taps


TAPS = kernel_taps(600)
TAIL = TAPS[2] / R_DECAY**2
FIRST = TAPS[1] + TAIL * R_DECAY


def split(values, terms):
    parts = []
    for _ in range(terms):
        part = values.astype(BF16)
        parts.append(part)
        values = values - part.astype(F32)
    return parts


def toeplitz(offset, rows, window):
    distance = offset + np.arange(rows)[:, None] - np.arange(window)[None, :]
    return (np.sign(distance) * TAPS[np.abs(distance)] / SCALE).astype(BF16)


def edge_state(rows, decay):
    return jnp.sum(rows * decay, 0, keepdims=True)


def edge_decay(lines, from_first):
    index = lax.broadcasted_iota(jnp.int32, (EDGE, ROWB), 0)
    steps = index + 1 if from_first else EDGE - index
    parity = 1.0 - 2.0 * (steps & 1).astype(F32)
    decay = parity * jnp.exp(steps.astype(F32) * math.log(R_DECAY))
    return jnp.concatenate([decay] * (lines // ROWB), 1)


def even_column():
    return lax.rem(lax.axis_index("gx"), 2) == 0


def neighbours(chip_ref, next_ref):
    is_even = even_column()
    chip, following = chip_ref[...], next_ref[...]
    return jnp.where(is_even, following, chip), jnp.where(is_even, chip, following)


def prep_body(x_cells, live, head, tail, cells, weights, offsets, request, to_chip, to_next):
    zero = jnp.zeros((2, head.shape[2]), F32)
    from_head, from_tail = edge_decay(head.shape[2], True), edge_decay(head.shape[2], False)
    to_left = jnp.concatenate(
        [edge_state(head[c], from_head) for c in range(3)] + [head[c, 0:1, :] for c in range(3)] + [zero], 0
    )
    to_right = jnp.concatenate(
        [edge_state(tail[c], from_tail) for c in range(3)]
        + [tail[c, EDGE - 1 : EDGE, :] for c in range(3)]
        + [zero],
        0,
    )
    is_even = even_column()
    to_chip[...] = jnp.where(is_even, to_right, to_left)
    to_next[...] = jnp.where(is_even, to_left, to_right)
    cell = cells[...]
    slots = cell.shape[1]
    row = jnp.floor((cell.astype(F32) + 0.5) * (1.0 / x_cells)).astype(jnp.int32)
    x = cell - row * x_cells
    line = row & (ROWB - 1)
    slot = (row >> 7)[0:1]
    lane = lax.broadcasted_iota(jnp.int32, (1, slots), 1)
    limit = jnp.zeros((1, slots), jnp.int32)
    counts = live[...].reshape(1, slots // PSIZE)
    for k in range(slots // PSIZE):
        limit = jnp.where(lane // PSIZE == k, counts[:, k : k + 1], limit)
    alive = lane % PSIZE < limit
    key = jnp.where(alive, slot, -1).astype(F32)
    w_high, w_low = split(weights[...], 2)
    o_high, o_low = split(offsets[...].reshape(1, slots), 2)
    request[...] = jnp.concatenate(
        [
            (x >> 3).astype(F32),
            (x & 7).astype(F32),
            line.astype(F32),
            w_high.astype(F32),
            w_low.astype(F32),
            o_high.astype(F32),
            o_low.astype(F32),
            key,
            jnp.zeros((9, slots), F32),
        ],
        0,
    ).astype(BF16)


def table_body(plan, v_ref, t_ref, held_ref, table_ref, sems):
    window = t_ref.shape[2]
    lines = v_ref.shape[2]
    width = 3 * ROWB
    copies = [pltpu.make_async_copy(v_ref.at[c], held_ref.at[c], sems.at[c]) for c in range(3)]
    for copy in copies:
        copy.start()
    for c in range(3):
        copies[c].wait()
        high = held_ref[c].astype(BF16)
        rows = [
            jnp.dot(t_ref[kind], high[start : start + window], preferred_element_type=F32)
            for row, start, kind in plan
        ]
        slopes = jnp.concatenate([(SCALE * r).astype(BF16) for r in rows], 0)
        for b in range(lines // ROWB):
            at = slice(b * ROWB, (b + 1) * ROWB)
            table_ref[b, c * ROWB : (c + 1) * ROWB] = jnp.transpose(high[:, at])
            table_ref[b, width + c * ROWB : width + (c + 1) * ROWB] = jnp.transpose(slopes[:, at])


def derivative_body(plan, v_ref, t_ref, sides_ref, g_ref, out_buf, sems):
    left, right = sides_ref[:8], sides_ref[8:]
    window = t_ref.shape[2]
    x_cells = v_ref.shape[1]
    copies = []
    for c in range(3):
        high, low = split(v_ref[c], 2)
        sent_to = 0
        for number, (row, start, kind) in enumerate(plan):
            matrix = t_ref[kind]
            both = jnp.concatenate([high[start : start + window], low[start : start + window]], 0)
            out = SCALE * jnp.dot(
                jnp.concatenate([matrix, matrix], 1), both, preferred_element_type=F32
            )
            out_buf[c, row : row + ROWS] = out
            if row == 0:
                out_buf[c, :EDGE] = edge_fix(out[:EDGE], left[c : c + 1], left[c + 3 : c + 4], True)
            if row + ROWS == x_cells:
                out_buf[c, x_cells - EDGE :] = edge_fix(
                    out_buf[c, x_cells - EDGE :], right[c : c + 1], right[c + 3 : c + 4], False
                )
            if number % 2 == 1 or row + ROWS == x_cells:
                rows = pl.ds(sent_to, row + ROWS - sent_to)
                sent_to = row + ROWS
                copy = pltpu.make_async_copy(
                    out_buf.at[c, rows], g_ref.at[c, rows], sems.at[len(copies)]
                )
                copy.start()
                copies.append(copy)
    for copy in copies:
        copy.wait()


def edge_fix(rows, state, plane, is_left):
    index = lax.broadcasted_iota(jnp.int32, rows.shape, 0)
    steps = index if is_left else EDGE - 1 - index
    parity = 1.0 - 2.0 * (steps & 1).astype(F32)
    decay = parity * jnp.exp(steps.astype(F32) * math.log(R_DECAY))
    sign = 1.0 if is_left else -1.0
    return rows + (sign * TAIL) * decay * state + jnp.where(steps == 0, sign * FIRST, 0.0) * plane


def signed_decay(steps):
    parity = 1.0 - 2.0 * (steps.astype(jnp.int32) & 1).astype(F32)
    return parity * jnp.exp(steps * math.log(R_DECAY))


def lookup_body(owners, xor, order, owner_ref, next_ref, chip_ref, table_ref, *refs):
    request_refs = refs[:owners]
    out_refs = refs[owners : 2 * owners]
    sides_ref = refs[2 * owners]
    requests, ranks, totals, states, peer_at = refs[2 * owners + 1 :]
    blocks, _, x_cells = table_ref.shape
    width = 3 * ROWB
    me = lax.axis_index("gy")
    capacity = blocks // 2
    slots = requests.shape[2]
    groups = slots // ROWB
    cells = STEN * CHUNK

    row_owners = owner_ref[...].astype(F32)
    row_lane = lax.broadcasted_iota(jnp.int32, row_owners.shape, 1)
    peers = []
    for block in range(blocks):
        mine = jnp.where(row_lane == me * blocks + block, row_owners, 0.0)
        owner = jnp.sum(mine).astype(jnp.int32)
        peers.append((owner ^ me) if xor else lax.rem(owner - me + owners, owners))
        peer_at[block] = peers[block]
    for k in range(owners):
        requests[order[k]] = request_refs[k][...]
        totals[k] = jnp.zeros(totals.shape[1:], F32)
    sides = jnp.concatenate(neighbours(chip_ref, next_ref), 0)
    sides_ref[...] = sides
    for block in range(blocks):
        states[block] = jnp.transpose(sides[:, block * ROWB : (block + 1) * ROWB]).astype(BF16)

    matched = []
    for block in range(blocks):
        rank = jnp.int32(0)
        for earlier in range(block):
            rank += (peers[earlier] == peers[block]).astype(jnp.int32)
        key = requests[peers[block], 16:32, :].astype(F32)[6:7]
        matched.append(jnp.where(key == (me * capacity + rank).astype(F32), 1.0, 0.0))
    stacked = jnp.concatenate(
        [m[:, k * ROWB : (k + 1) * ROWB] for m in matched for k in range(groups)], 0
    )
    upto = lax.broadcasted_iota(jnp.int32, (ROWB, ROWB), 0) <= lax.broadcasted_iota(
        jnp.int32, (ROWB, ROWB), 1
    )
    running = jnp.dot(
        stacked.astype(BF16), jnp.where(upto, 1.0, 0.0).astype(BF16), preferred_element_type=F32
    )
    ends = []
    end = jnp.int32(0)
    for block in range(blocks):
        before = jnp.zeros((1, 1), F32)
        pieces = []
        for k in range(groups):
            r = block * groups + k
            line = running[r : r + 1]
            pieces.append(jnp.where(stacked[r : r + 1] > 0.5, line - 1.0 + before, -1.0))
            before = before + line[:, ROWB - 1 : ROWB]
        ranks[block] = jnp.concatenate(pieces, 1)
        count = before[0, 0].astype(jnp.int32)
        end = end + jnp.maximum((count + CHUNK - 1) // CHUNK - 1, 0)
        ends.append(end)

    x_iota = lax.broadcasted_iota(jnp.int32, (x_cells, cells), 0).astype(F32)
    line_iota = lax.broadcasted_iota(jnp.int32, (ROWB, cells), 0).astype(F32)
    state_iota = lax.broadcasted_iota(jnp.int32, (16, cells), 0)
    place = lax.broadcasted_iota(jnp.int32, (CHUNK, slots), 0)
    low_half = lax.broadcasted_iota(jnp.int32, (1, 2 * CHUNK), 1) < CHUNK

    def batch(tasks):
        chosen, data = [], []
        for block, peer, i in tasks:
            one = jnp.where(ranks[block] == (place + i * CHUNK).astype(F32), 1.0, 0.0).astype(BF16)
            chosen.append(jnp.concatenate([one, one], 0))
        for (block, peer, i), pick in zip(tasks, chosen):
            data.append(
                lax.dot_general(
                    requests[peer], pick, (((1,), (1,)), ((), ())), preferred_element_type=F32
                )
            )
        found, halos, masks, offsets = [], [], [], []
        for (block, peer, i), d in zip(tasks, data):

            def by_cell(row):
                pairs = [
                    jnp.where(low_half, d[row + s : row + s + 1], d[row + s + 1 : row + s + 2])
                    for s in (0, 2)
                ]
                return jnp.concatenate(pairs, 1)

            x = by_cell(0) * 8.0 + by_cell(4)
            weight = by_cell(12) + by_cell(16)
            offset = d[20:21] + d[21:22]
            offsets.append(jnp.concatenate([offset, offset], 1))
            masks.append(jnp.where(line_iota == by_cell(8), weight, 0.0))
            pick = jnp.where(x_iota == x, 1.0, 0.0).astype(BF16)
            found.append(jnp.dot(table_ref[block], pick, preferred_element_type=F32))
            y = x_cells - 1.0 - x
            left = jnp.where(x < EDGE, TAIL * signed_decay(x), 0.0)
            right = jnp.where(y < EDGE, -TAIL * signed_decay(y), 0.0)
            left_first = jnp.where(x == 0.0, FIRST, 0.0)
            right_first = jnp.where(y == 0.0, -FIRST, 0.0)
            terms = []
            for c in range(3):
                term = jnp.where(state_iota == c, left, 0.0)
                term = jnp.where(state_iota == c + 3, left_first, term)
                term = jnp.where(state_iota == c + 8, right, term)
                terms.append(jnp.where(state_iota == c + 11, right_first, term))
            halos.append(
                jnp.dot(
                    states[block],
                    jnp.concatenate(terms, 1).astype(BF16),
                    preferred_element_type=F32,
                )
            )
        for (block, peer, i), f, h, mask, offset, pick in zip(
            tasks, found, halos, masks, offsets, chosen
        ):
            sums = []
            for c in range(3):
                carried = f[c * ROWB : (c + 1) * ROWB]
                slope = f[width + c * ROWB : width + (c + 1) * ROWB]
                slope = slope + h[:, c * cells : (c + 1) * cells]
                sums.append(jnp.sum((carried + offset * slope) * mask, 0, keepdims=True))
            sums.append(jnp.zeros((1, cells), F32))
            value = jnp.concatenate(sums, 0)
            value = value[:, : 2 * CHUNK] + value[:, 2 * CHUNK :]
            back = jnp.concatenate(
                [p.astype(F32) for p in split(value, 3)] + [jnp.zeros((4, 2 * CHUNK), F32)], 0
            )
            totals[peer] += jnp.dot(back.astype(BF16), pick, preferred_element_type=F32)

    def extra(number):
        block = jnp.int32(0)
        first = jnp.int32(0)
        for b in range(blocks - 1):
            past = number >= ends[b]
            block = jnp.where(past, b + 1, block)
            first = jnp.where(past, ends[b], first)
        return block, peer_at[block], number - first + 1

    base = [(block, peers[block], jnp.int32(0)) for block in range(blocks)]
    extras = ends[-1]
    sizes = [0, EXTRA, 2 * EXTRA]
    for size, above in zip(sizes, sizes[1:] + [None]):
        fits = extras > size - EXTRA
        if above is not None:
            fits = jnp.logical_and(fits, extras <= size)

        @pl.when(fits)
        def _(size=size):
            batch(base + [extra(jnp.int32(t)) for t in range(size)])

    @pl.loop(2, (extras + EXTRA - 1) // EXTRA)
    def _(i):
        batch([extra(i * EXTRA + t) for t in range(EXTRA)])

    for k in range(owners):
        total = totals[k]
        out_refs[k][...] = total[0:8] + pltpu.roll(total[0:8], 4, 0) + total[8:16]


def final_body(request, relax, particle, *refs):
    parts, (fluid_ref, updated_ref) = refs[:-2], refs[-2:]
    raw = parts[0][0:3]
    for part in parts[1:]:
        raw = raw + part[0:3]
    slots = raw.shape[1]
    alive = jnp.broadcast_to(request[16:32].astype(F32)[6:7], raw.shape) >= 0.0
    fluid = jnp.where(alive, raw, 0.0)
    velocity = particle[...]
    fluid_ref[...] = fluid
    updated_ref[...] = jnp.where(
        alive, velocity + relax[...].reshape(1, slots) * (fluid - velocity), velocity
    )


def sent(values, axis, pairs):
    return lax.ppermute(values, axis, pairs)


def per_device(
    velocity, row_owner, cell_list, weights, offsets, relax_rate, particle_velocity, live_counts
):
    components, x_cells, lines = velocity.shape
    slots = weights.shape[1]
    columns = lax.axis_size("gx")
    owners = lax.axis_size("gy")
    blocks = lines // ROWB
    xor = owners & (owners - 1) == 0
    vmem = pl.BlockSpec(memory_space=pltpu.VMEM)
    smem = pl.BlockSpec(memory_space=pltpu.SMEM)
    hbm = pl.BlockSpec(memory_space=pltpu.HBM)
    limit = 24 * 1024 * 1024
    one = lambda shape: pl.BlockSpec(shape, lambda i: (0,) * len(shape))

    last = x_cells // EDGE - 1
    request, to_chip, to_next = pl.pallas_call(
        lambda *refs: prep_body(x_cells, *refs),
        grid=(1,),
        in_specs=[
            one((slots // PSIZE,)),
            pl.BlockSpec((3, EDGE, lines), lambda i: (0, 0, 0)),
            pl.BlockSpec((3, EDGE, lines), lambda i: (0, last, 0)),
            one((STEN, slots)),
            one((STEN, slots)),
            one((slots,)),
        ],
        out_specs=[vmem] * 3,
        out_shape=[
            jax.ShapeDtypeStruct((32, slots), BF16),
            jax.ShapeDtypeStruct((8, lines), F32),
            jax.ShapeDtypeStruct((8, lines), F32),
        ],
        name="prepare",
    )(live_counts, velocity, velocity, cell_list, weights, offsets)

    after = [(i + 1) % columns if i % 2 else (i - 1) % columns for i in range(columns)]
    from_next = sent(to_next, "gx", [(i, after[i]) for i in range(columns)])
    from_chip = sent(to_chip, "gx", [(i, i ^ 1) for i in range(columns)])

    def peer(i, k):
        return i ^ k if xor else (i + k) % owners

    far_first = sorted(range(1, owners), key=lambda k: -bin(k).count("1"))
    requests = [request] + [
        sent(request, "gy", [(peer(i, k), i) for i in range(owners)]) for k in far_first
    ]

    window = min(256, x_cells)
    plan, kinds = [], []
    for row in range(0, x_cells, ROWS):
        start = min(max(row - 32, 0), x_cells - window)
        if row - start not in kinds:
            kinds.append(row - start)
        plan.append((row, start, kinds.index(row - start)))
    matrices = jnp.asarray(np.stack([toeplitz(o, ROWS, window) for o in kinds]))
    width = 3 * ROWB
    held, table = pl.pallas_call(
        lambda *refs: table_body(plan, *refs),
        in_specs=[hbm, vmem],
        out_specs=[vmem, vmem],
        out_shape=[
            jax.ShapeDtypeStruct(velocity.shape, F32),
            jax.ShapeDtypeStruct((blocks, 2 * width, x_cells), BF16),
        ],
        scratch_shapes=[pltpu.SemaphoreType.DMA((3,))],
        compiler_params=pltpu.CompilerParams(vmem_limit_bytes=LOAD * 1024 * 1024),
        cost_estimate=pl.CostEstimate(
            flops=2 * window * velocity.size, bytes_accessed=8 * velocity.size, transcendentals=0
        ),
        name="table",
    )(velocity, matrices)

    *partials, sides = pl.pallas_call(
        lambda *refs: lookup_body(owners, xor, [0] + far_first, *refs),
        in_specs=[vmem] * (4 + owners),
        out_specs=[vmem] * (owners + 1),
        out_shape=[jax.ShapeDtypeStruct((8, slots), F32)] * owners
        + [jax.ShapeDtypeStruct((16, lines), F32)],
        scratch_shapes=[
            pltpu.VMEM((owners, 32, slots), BF16),
            pltpu.VMEM((blocks, 1, slots), F32),
            pltpu.VMEM((owners, 16, slots), F32),
            pltpu.VMEM((blocks, ROWB, 16), BF16),
            pltpu.SMEM((blocks,), jnp.int32),
        ],
        compiler_params=pltpu.CompilerParams(vmem_limit_bytes=limit),
        cost_estimate=pl.CostEstimate(
            flops=2 * 768 * 6 * x_cells * 1024, bytes_accessed=2 * velocity.size, transcendentals=0
        ),
        name="lookup",
    )(row_owner, from_next, from_chip, table, *requests)

    gradient = pl.pallas_call(
        lambda *refs: derivative_body(plan, *refs),
        in_specs=[vmem] * 3,
        out_specs=hbm,
        out_shape=jax.ShapeDtypeStruct(velocity.shape, F32),
        scratch_shapes=[
            pltpu.VMEM(velocity.shape, F32),
            pltpu.SemaphoreType.DMA((3 * len(plan),)),
        ],
        compiler_params=pltpu.CompilerParams(vmem_limit_bytes=limit),
        cost_estimate=pl.CostEstimate(
            flops=6 * window * velocity.size, bytes_accessed=8 * velocity.size, transcendentals=0
        ),
        name="derivative",
    )(held, matrices, sides)

    returned = [partials[0]] + [
        sent(partials[k], "gy", [(i, peer(i, k)) for i in range(owners)]) for k in far_first
    ]
    shape = jax.ShapeDtypeStruct((3, slots), F32)
    fluid, updated = pl.pallas_call(
        final_body,
        in_specs=[vmem] * (3 + owners),
        out_specs=[vmem] * 2,
        out_shape=[shape, shape],
        compiler_params=pltpu.CompilerParams(vmem_limit_bytes=limit),
        name="finish",
    )(request, relax_rate, particle_velocity, *returned)
    return (gradient, fluid, updated)


def solution(mesh):
    return jax.shard_map(
        per_device,
        mesh=mesh,
        in_specs=(
            P(None, "gx", "gy"),
            P("gx", None),
            P(None, ("gx", "gy")),
            P(None, ("gx", "gy")),
            P(("gx", "gy")),
            P(("gx", "gy")),
            P(None, ("gx", "gy")),
            P(("gx", "gy")),
        ),
        out_specs=(P(None, "gx", "gy"), P(None, ("gx", "gy")), P(None, ("gx", "gy"))),
        check_vma=False,
    )
```

```python
import math

import jax
import jax.numpy as jnp
import numpy as np
from jax import lax
from jax.experimental import pallas as pl
from jax.experimental.pallas import tpu as pltpu
from jax.sharding import PartitionSpec as P

ROWB = 128
PSIZE = 128
STEN = 4
EDGE = 32
ROWS = 192
CHUNK = 64
EXTRA = 2
LOAD = 43
SCALE = 1.95685
R_DECAY = (3.0 - math.sqrt(5.0)) / 2.0
F32 = jnp.float32
BF16 = jnp.bfloat16


def kernel_taps(reach):
    level = 3.0 / math.sqrt(5.0)

    def inverse(n):
        return level * (-R_DECAY) ** abs(n)

    taps = np.zeros(reach + 1)
    for n in range(reach + 1):
        taps[n] = (7.0 / 9.0) * (inverse(n + 1) - inverse(n - 1)) + (1.0 / 36.0) * (
            inverse(n + 2) - inverse(n - 2)
        )
    return taps


TAPS = kernel_taps(600)
TAIL = TAPS[2] / R_DECAY**2
FIRST = TAPS[1] + TAIL * R_DECAY


def split(values, terms):
    parts = []
    for _ in range(terms):
        part = values.astype(BF16)
        parts.append(part)
        values = values - part.astype(F32)
    return parts


def toeplitz(offset, rows, window):
    distance = offset + np.arange(rows)[:, None] - np.arange(window)[None, :]
    return (np.sign(distance) * TAPS[np.abs(distance)] / SCALE).astype(BF16)


def edge_state(rows, from_first):
    index = lax.broadcasted_iota(jnp.int32, rows.shape, 0)
    steps = index + 1 if from_first else EDGE - index
    parity = 1.0 - 2.0 * (steps & 1).astype(F32)
    decay = parity * jnp.exp(steps.astype(F32) * math.log(R_DECAY))
    return jnp.sum(rows * decay, 0, keepdims=True)


def even_column():
    return lax.rem(lax.axis_index("gx"), 2) == 0


def neighbours(chip_ref, next_ref):
    is_even = even_column()
    chip, following = chip_ref[...], next_ref[...]
    return jnp.where(is_even, following, chip), jnp.where(is_even, chip, following)


def prep_body(x_cells, live, head, tail, cells, weights, offsets, request, to_chip, to_next):
    zero = jnp.zeros((2, head.shape[2]), F32)
    to_left = jnp.concatenate(
        [edge_state(head[c], True) for c in range(3)] + [head[c, 0:1, :] for c in range(3)] + [zero], 0
    )
    to_right = jnp.concatenate(
        [edge_state(tail[c], False) for c in range(3)]
        + [tail[c, EDGE - 1 : EDGE, :] for c in range(3)]
        + [zero],
        0,
    )
    is_even = even_column()
    to_chip[...] = jnp.where(is_even, to_right, to_left)
    to_next[...] = jnp.where(is_even, to_left, to_right)
    cell = cells[...]
    slots = cell.shape[1]
    row = jnp.floor((cell.astype(F32) + 0.5) * (1.0 / x_cells)).astype(jnp.int32)
    x = cell - row * x_cells
    line = row & (ROWB - 1)
    slot = (row >> 7)[0:1]
    lane = lax.broadcasted_iota(jnp.int32, (1, slots), 1)
    limit = jnp.zeros((1, slots), jnp.int32)
    counts = live[...].reshape(1, slots // PSIZE)
    for k in range(slots // PSIZE):
        limit = jnp.where(lane // PSIZE == k, counts[:, k : k + 1], limit)
    alive = lane % PSIZE < limit
    key = jnp.where(alive, slot, -1).astype(F32)
    w_high, w_low = split(weights[...], 2)
    o_high, o_low = split(offsets[...].reshape(1, slots), 2)
    request[...] = jnp.concatenate(
        [
            (x >> 3).astype(F32),
            (x & 7).astype(F32),
            line.astype(F32),
            w_high.astype(F32),
            w_low.astype(F32),
            o_high.astype(F32),
            o_low.astype(F32),
            key,
            jnp.zeros((9, slots), F32),
        ],
        0,
    ).astype(BF16)


def table_body(plan, v_ref, t_ref, held_ref, table_ref, sems):
    window = t_ref.shape[2]
    lines = v_ref.shape[2]
    width = 3 * ROWB
    copies = [pltpu.make_async_copy(v_ref.at[c], held_ref.at[c], sems.at[c]) for c in range(3)]
    for copy in copies:
        copy.start()
    for c in range(3):
        copies[c].wait()
        high = held_ref[c].astype(BF16)
        rows = [
            jnp.dot(t_ref[kind], high[start : start + window], preferred_element_type=F32)
            for row, start, kind in plan
        ]
        slopes = jnp.concatenate([(SCALE * r).astype(BF16) for r in rows], 0)
        for b in range(lines // ROWB):
            at = slice(b * ROWB, (b + 1) * ROWB)
            table_ref[b, c * ROWB : (c + 1) * ROWB] = jnp.transpose(high[:, at])
            table_ref[b, width + c * ROWB : width + (c + 1) * ROWB] = jnp.transpose(slopes[:, at])


def derivative_body(plan, v_ref, t_ref, sides_ref, g_ref, out_buf, sems):
    left, right = sides_ref[:8], sides_ref[8:]
    window = t_ref.shape[2]
    x_cells = v_ref.shape[1]
    copies = []
    for c in range(3):
        high, low = split(v_ref[c], 2)
        sent_to = 0
        for number, (row, start, kind) in enumerate(plan):
            matrix = t_ref[kind]
            both = jnp.concatenate([high[start : start + window], low[start : start + window]], 0)
            out = SCALE * jnp.dot(
                jnp.concatenate([matrix, matrix], 1), both, preferred_element_type=F32
            )
            out_buf[c, row : row + ROWS] = out
            if row == 0:
                out_buf[c, :EDGE] = edge_fix(out[:EDGE], left[c : c + 1], left[c + 3 : c + 4], True)
            if row + ROWS == x_cells:
                out_buf[c, x_cells - EDGE :] = edge_fix(
                    out_buf[c, x_cells - EDGE :], right[c : c + 1], right[c + 3 : c + 4], False
                )
            if number % 2 == 1 or row + ROWS == x_cells:
                rows = pl.ds(sent_to, row + ROWS - sent_to)
                sent_to = row + ROWS
                copy = pltpu.make_async_copy(
                    out_buf.at[c, rows], g_ref.at[c, rows], sems.at[len(copies)]
                )
                copy.start()
                copies.append(copy)
    for copy in copies:
        copy.wait()


def edge_fix(rows, state, plane, is_left):
    index = lax.broadcasted_iota(jnp.int32, rows.shape, 0)
    steps = index if is_left else EDGE - 1 - index
    parity = 1.0 - 2.0 * (steps & 1).astype(F32)
    decay = parity * jnp.exp(steps.astype(F32) * math.log(R_DECAY))
    sign = 1.0 if is_left else -1.0
    return rows + (sign * TAIL) * decay * state + jnp.where(steps == 0, sign * FIRST, 0.0) * plane


def signed_decay(steps):
    parity = 1.0 - 2.0 * (steps.astype(jnp.int32) & 1).astype(F32)
    return parity * jnp.exp(steps * math.log(R_DECAY))


def lookup_body(owners, xor, order, owner_ref, next_ref, chip_ref, table_ref, *refs):
    request_refs = refs[:owners]
    out_refs = refs[owners : 2 * owners]
    sides_ref = refs[2 * owners]
    requests, ranks, totals, states, peer_at = refs[2 * owners + 1 :]
    blocks, _, x_cells = table_ref.shape
    width = 3 * ROWB
    me = lax.axis_index("gy")
    capacity = blocks // 2
    slots = requests.shape[2]
    groups = slots // ROWB
    cells = STEN * CHUNK

    row_owners = owner_ref[...].astype(F32)
    row_lane = lax.broadcasted_iota(jnp.int32, row_owners.shape, 1)
    peers = []
    for block in range(blocks):
        mine = jnp.where(row_lane == me * blocks + block, row_owners, 0.0)
        owner = jnp.sum(mine).astype(jnp.int32)
        peers.append((owner ^ me) if xor else lax.rem(owner - me + owners, owners))
        peer_at[block] = peers[block]
    for k in range(owners):
        requests[order[k]] = request_refs[k][...]
        totals[k] = jnp.zeros(totals.shape[1:], F32)
    sides = jnp.concatenate(neighbours(chip_ref, next_ref), 0)
    sides_ref[...] = sides
    for block in range(blocks):
        states[block] = jnp.transpose(sides[:, block * ROWB : (block + 1) * ROWB]).astype(BF16)

    matched = []
    for block in range(blocks):
        rank = jnp.int32(0)
        for earlier in range(block):
            rank += (peers[earlier] == peers[block]).astype(jnp.int32)
        key = requests[peers[block], 16:32, :].astype(F32)[6:7]
        matched.append(jnp.where(key == (me * capacity + rank).astype(F32), 1.0, 0.0))
    stacked = jnp.concatenate(
        [m[:, k * ROWB : (k + 1) * ROWB] for m in matched for k in range(groups)], 0
    )
    upto = lax.broadcasted_iota(jnp.int32, (ROWB, ROWB), 0) <= lax.broadcasted_iota(
        jnp.int32, (ROWB, ROWB), 1
    )
    running = jnp.dot(
        stacked.astype(BF16), jnp.where(upto, 1.0, 0.0).astype(BF16), preferred_element_type=F32
    )
    ends = []
    end = jnp.int32(0)
    for block in range(blocks):
        before = jnp.zeros((1, 1), F32)
        pieces = []
        for k in range(groups):
            r = block * groups + k
            line = running[r : r + 1]
            pieces.append(jnp.where(stacked[r : r + 1] > 0.5, line - 1.0 + before, -1.0))
            before = before + line[:, ROWB - 1 : ROWB]
        ranks[block] = jnp.concatenate(pieces, 1)
        count = before[0, 0].astype(jnp.int32)
        end = end + jnp.maximum((count + CHUNK - 1) // CHUNK - 1, 0)
        ends.append(end)

    x_iota = lax.broadcasted_iota(jnp.int32, (x_cells, cells), 0).astype(F32)
    line_iota = lax.broadcasted_iota(jnp.int32, (ROWB, cells), 0).astype(F32)
    state_iota = lax.broadcasted_iota(jnp.int32, (16, cells), 0)
    place = lax.broadcasted_iota(jnp.int32, (CHUNK, slots), 0)
    low_half = lax.broadcasted_iota(jnp.int32, (1, 2 * CHUNK), 1) < CHUNK

    def batch(tasks):
        chosen, data = [], []
        for block, peer, i in tasks:
            one = jnp.where(ranks[block] == (place + i * CHUNK).astype(F32), 1.0, 0.0).astype(BF16)
            chosen.append(jnp.concatenate([one, one], 0))
        for (block, peer, i), pick in zip(tasks, chosen):
            data.append(
                lax.dot_general(
                    requests[peer], pick, (((1,), (1,)), ((), ())), preferred_element_type=F32
                )
            )
        found, halos, masks, offsets = [], [], [], []
        for (block, peer, i), d in zip(tasks, data):

            def by_cell(row):
                pairs = [
                    jnp.where(low_half, d[row + s : row + s + 1], d[row + s + 1 : row + s + 2])
                    for s in (0, 2)
                ]
                return jnp.concatenate(pairs, 1)

            x = by_cell(0) * 8.0 + by_cell(4)
            weight = by_cell(12) + by_cell(16)
            offset = d[20:21] + d[21:22]
            offsets.append(jnp.concatenate([offset, offset], 1))
            masks.append(jnp.where(line_iota == by_cell(8), weight, 0.0))
            pick = jnp.where(x_iota == x, 1.0, 0.0).astype(BF16)
            found.append(jnp.dot(table_ref[block], pick, preferred_element_type=F32))
            y = x_cells - 1.0 - x
            left = jnp.where(x < EDGE, TAIL * signed_decay(x), 0.0)
            right = jnp.where(y < EDGE, -TAIL * signed_decay(y), 0.0)
            left_first = jnp.where(x == 0.0, FIRST, 0.0)
            right_first = jnp.where(y == 0.0, -FIRST, 0.0)
            terms = []
            for c in range(3):
                term = jnp.where(state_iota == c, left, 0.0)
                term = jnp.where(state_iota == c + 3, left_first, term)
                term = jnp.where(state_iota == c + 8, right, term)
                terms.append(jnp.where(state_iota == c + 11, right_first, term))
            halos.append(
                jnp.dot(
                    states[block],
                    jnp.concatenate(terms, 1).astype(BF16),
                    preferred_element_type=F32,
                )
            )
        for (block, peer, i), f, h, mask, offset, pick in zip(
            tasks, found, halos, masks, offsets, chosen
        ):
            sums = []
            for c in range(3):
                carried = f[c * ROWB : (c + 1) * ROWB]
                slope = f[width + c * ROWB : width + (c + 1) * ROWB]
                slope = slope + h[:, c * cells : (c + 1) * cells]
                sums.append(jnp.sum((carried + offset * slope) * mask, 0, keepdims=True))
            sums.append(jnp.zeros((1, cells), F32))
            value = jnp.concatenate(sums, 0)
            value = value[:, : 2 * CHUNK] + value[:, 2 * CHUNK :]
            back = jnp.concatenate(
                [p.astype(F32) for p in split(value, 3)] + [jnp.zeros((4, 2 * CHUNK), F32)], 0
            )
            totals[peer] += jnp.dot(back.astype(BF16), pick, preferred_element_type=F32)

    def extra(number):
        block = jnp.int32(0)
        first = jnp.int32(0)
        for b in range(blocks - 1):
            past = number >= ends[b]
            block = jnp.where(past, b + 1, block)
            first = jnp.where(past, ends[b], first)
        return block, peer_at[block], number - first + 1

    base = [(block, peers[block], jnp.int32(0)) for block in range(blocks)]
    extras = ends[-1]
    sizes = [0, EXTRA, 2 * EXTRA]
    for size, above in zip(sizes, sizes[1:] + [None]):
        fits = extras > size - EXTRA
        if above is not None:
            fits = jnp.logical_and(fits, extras <= size)

        @pl.when(fits)
        def _(size=size):
            batch(base + [extra(jnp.int32(t)) for t in range(size)])

    @pl.loop(2, (extras + EXTRA - 1) // EXTRA)
    def _(i):
        batch([extra(i * EXTRA + t) for t in range(EXTRA)])

    for k in range(owners):
        total = totals[k]
        out_refs[k][...] = total[0:8] + pltpu.roll(total[0:8], 4, 0) + total[8:16]


def final_body(request, relax, particle, *refs):
    parts, (fluid_ref, updated_ref) = refs[:-2], refs[-2:]
    raw = parts[0][0:3]
    for part in parts[1:]:
        raw = raw + part[0:3]
    slots = raw.shape[1]
    alive = jnp.broadcast_to(request[16:32].astype(F32)[6:7], raw.shape) >= 0.0
    fluid = jnp.where(alive, raw, 0.0)
    velocity = particle[...]
    fluid_ref[...] = fluid
    updated_ref[...] = jnp.where(
        alive, velocity + relax[...].reshape(1, slots) * (fluid - velocity), velocity
    )


def sent(values, axis, pairs):
    return lax.ppermute(values, axis, pairs)


def per_device(
    velocity, row_owner, cell_list, weights, offsets, relax_rate, particle_velocity, live_counts
):
    components, x_cells, lines = velocity.shape
    slots = weights.shape[1]
    columns = lax.axis_size("gx")
    owners = lax.axis_size("gy")
    blocks = lines // ROWB
    xor = owners & (owners - 1) == 0
    vmem = pl.BlockSpec(memory_space=pltpu.VMEM)
    smem = pl.BlockSpec(memory_space=pltpu.SMEM)
    hbm = pl.BlockSpec(memory_space=pltpu.HBM)
    limit = 24 * 1024 * 1024
    one = lambda shape: pl.BlockSpec(shape, lambda i: (0,) * len(shape))

    last = x_cells // EDGE - 1
    request, to_chip, to_next = pl.pallas_call(
        lambda *refs: prep_body(x_cells, *refs),
        grid=(1,),
        in_specs=[
            one((slots // PSIZE,)),
            pl.BlockSpec((3, EDGE, lines), lambda i: (0, 0, 0)),
            pl.BlockSpec((3, EDGE, lines), lambda i: (0, last, 0)),
            one((STEN, slots)),
            one((STEN, slots)),
            one((slots,)),
        ],
        out_specs=[vmem] * 3,
        out_shape=[
            jax.ShapeDtypeStruct((32, slots), BF16),
            jax.ShapeDtypeStruct((8, lines), F32),
            jax.ShapeDtypeStruct((8, lines), F32),
        ],
        name="prepare",
    )(live_counts, velocity, velocity, cell_list, weights, offsets)

    after = [(i + 1) % columns if i % 2 else (i - 1) % columns for i in range(columns)]
    from_next = sent(to_next, "gx", [(i, after[i]) for i in range(columns)])
    from_chip = sent(to_chip, "gx", [(i, i ^ 1) for i in range(columns)])

    def peer(i, k):
        return i ^ k if xor else (i + k) % owners

    far_first = sorted(range(1, owners), key=lambda k: -bin(k).count("1"))
    requests = [request] + [
        sent(request, "gy", [(peer(i, k), i) for i in range(owners)]) for k in range(1, owners)
    ]

    window = min(256, x_cells)
    plan, kinds = [], []
    for row in range(0, x_cells, ROWS):
        start = min(max(row - EDGE, 0), x_cells - window)
        if row - start not in kinds:
            kinds.append(row - start)
        plan.append((row, start, kinds.index(row - start)))
    matrices = jnp.asarray(np.stack([toeplitz(o, ROWS, window) for o in kinds]))
    width = 3 * ROWB
    held, table = pl.pallas_call(
        lambda *refs: table_body(plan, *refs),
        in_specs=[hbm, vmem],
        out_specs=[vmem, vmem],
        out_shape=[
            jax.ShapeDtypeStruct(velocity.shape, F32),
            jax.ShapeDtypeStruct((blocks, 2 * width, x_cells), BF16),
        ],
        scratch_shapes=[pltpu.SemaphoreType.DMA((3,))],
        compiler_params=pltpu.CompilerParams(vmem_limit_bytes=LOAD * 1024 * 1024),
        cost_estimate=pl.CostEstimate(
            flops=2 * window * velocity.size, bytes_accessed=8 * velocity.size, transcendentals=0
        ),
        name="table",
    )(velocity, matrices)

    *partials, sides = pl.pallas_call(
        lambda *refs: lookup_body(owners, xor, list(range(owners)), *refs),
        in_specs=[vmem] * (4 + owners),
        out_specs=[vmem] * (owners + 1),
        out_shape=[jax.ShapeDtypeStruct((8, slots), F32)] * owners
        + [jax.ShapeDtypeStruct((16, lines), F32)],
        scratch_shapes=[
            pltpu.VMEM((owners, 32, slots), BF16),
            pltpu.VMEM((blocks, 1, slots), F32),
            pltpu.VMEM((owners, 16, slots), F32),
            pltpu.VMEM((blocks, ROWB, 16), BF16),
            pltpu.SMEM((blocks,), jnp.int32),
        ],
        compiler_params=pltpu.CompilerParams(vmem_limit_bytes=limit),
        cost_estimate=pl.CostEstimate(
            flops=2 * 768 * 6 * x_cells * 1024, bytes_accessed=2 * velocity.size, transcendentals=0
        ),
        name="lookup",
    )(row_owner, from_next, from_chip, table, *requests)

    gradient = pl.pallas_call(
        lambda *refs: derivative_body(plan, *refs),
        in_specs=[vmem] * 3,
        out_specs=hbm,
        out_shape=jax.ShapeDtypeStruct(velocity.shape, F32),
        scratch_shapes=[
            pltpu.VMEM(velocity.shape, F32),
            pltpu.SemaphoreType.DMA((3 * len(plan),)),
        ],
        compiler_params=pltpu.CompilerParams(vmem_limit_bytes=limit),
        cost_estimate=pl.CostEstimate(
            flops=6 * window * velocity.size, bytes_accessed=8 * velocity.size, transcendentals=0
        ),
        name="derivative",
    )(held, matrices, sides)

    returned = [partials[0]] + [
        sent(partials[k], "gy", [(i, peer(i, k)) for i in range(owners)]) for k in far_first
    ]
    shape = jax.ShapeDtypeStruct((3, slots), F32)
    fluid, updated = pl.pallas_call(
        final_body,
        in_specs=[vmem] * (3 + owners),
        out_specs=[vmem] * 2,
        out_shape=[shape, shape],
        compiler_params=pltpu.CompilerParams(vmem_limit_bytes=limit),
        name="finish",
    )(request, relax_rate, particle_velocity, *returned)
    return (gradient, fluid, updated)


def solution(mesh):
    return jax.shard_map(
        per_device,
        mesh=mesh,
        in_specs=(
            P(None, "gx", "gy"),
            P("gx", None),
            P(None, ("gx", "gy")),
            P(None, ("gx", "gy")),
            P(("gx", "gy")),
            P(("gx", "gy")),
            P(None, ("gx", "gy")),
            P(("gx", "gy")),
        ),
        out_specs=(P(None, "gx", "gy"), P(None, ("gx", "gy")), P(None, ("gx", "gy"))),
        check_vma=False,
    )
```
